32 devices in a mesh: groups: 2 (over x), gx: 8 (over z, y), gy: 2 (over core).
Axes of the slice: x: 2, y: 2, z: 4, core: 2. Of those that a mesh axis runs over, the one named last changes fastest.
Arguments:
- tokens: bfloat16 [64, 16384], P('groups', 'gx'), parts along dimension 0, may hold values from -6 to 6
- w_query: bfloat16 [16384, 8192], P('gx', 'gy'), may hold values from -0.046875 to 0.046875
- w_key: bfloat16 [16384, 512], P('gx', 'gy'), may hold values from -0.046875 to 0.046875
- w_value: bfloat16 [16384, 512], P('gx', 'gy'), may hold values from -0.046875 to 0.046875
- w_out: bfloat16 [8192, 16384], P('gy', 'gx'), may hold values from -0.0625 to 0.0625
- key_cache: bfloat16 [64, 4, 1024, 128], P(('groups', 'gx'), 'gy'), parts along dimension 0, may hold values from -600 to 600
- value_cache: bfloat16 [64, 4, 1024, 128], P(('groups', 'gx'), 'gy'), parts along dimension 0, may hold values from -6 to 6
- lengths: int32 [64], P(('groups', 'gx')), parts along dimension 0, may hold values from 2 to 1024, as said below
Outputs:
- attended: bfloat16 [64, 16384], P(('groups', 'gy'), 'gx'), parts along dimension 0
The draws below stay inside these ranges and needn't reach their ends.
There are 2 independent parts, one for each index of `groups`. The reference program is written for one: setup_inputs(seed, part) draws one part's arguments, and reference() takes and returns one part's arrays. A program takes and returns all parts, laid end to end along the dimension named above; an argument that names none is the same for every part. Nothing has to cross between parts.
Inputs may be any that keep to these rules, and one draw needn't show every extreme that they name: `lengths`: every row has 2 or more filled slots; some row has all 1024 slots filled.
All inputs are finite; a program needn't handle non-finite values.
Results may differ from the reference program's by a relative error of at most 0.011.
Values may be sent and summed in bfloat16 or wider, within the bound.
No kernel may reach another device: no remote copies, remote signals or barrier semaphores. Data moves between devices by JAX's collectives and lax.ppermute only.
A program may use at most 128 MiB of HBM per device.

```python
import jax
import jax.numpy as jnp
from jax import lax

D = 16384
HQ = 64
KVH = 4
HD = 128
CACHE = 1024
BATCH = 32


def draw_key_cache(key, part):
    base = jax.random.normal(key, (BATCH, KVH, CACHE, HD), jnp.float32)
    base = jnp.clip(base, -5.0, 5.0)
    return jnp.clip(base, -600.0, 600.0).astype(jnp.bfloat16)


def draw_lengths(key, part):
    sampled = jax.random.randint(key, (BATCH,), 2, CACHE + 1, dtype=jnp.int32)
    longest = jax.random.randint(jax.random.fold_in(key, 7), (), 0, BATCH, dtype=jnp.int32)
    return sampled.at[longest].set(CACHE)


def level_of(stream_key, shape, cuts, low, high):
    gain = 1.0
    for dim, blocks in cuts:
        heights = jax.random.uniform(jax.random.fold_in(jax.random.fold_in(stream_key, 6), dim), (blocks,), jnp.float32, low / len(cuts), high / len(cuts))
        gain = gain * jnp.repeat(jnp.exp(heights), shape[dim] // blocks).reshape((-1,) + (1,) * (len(shape) - 1 - dim))
    return gain


def noise(key, dims, spread, most, pieces=(), held_as=jnp.bfloat16):
    entries = jax.random.normal(key, dims, jnp.float32) * spread
    if len(pieces) > 0:
        entries = level_of(key, dims, pieces, -0.22, 0.18) * entries
    return jnp.clip(entries, min=-most, max=most).astype(held_as)


def setup_inputs(seed: int = 0, part: int = 0) -> dict:
    streams_of = jax.random.split(jax.random.key(seed), 9)
    part_keys = jax.random.split(jax.random.fold_in(streams_of[8], part), 9)
    return {
        "tokens": noise(part_keys[0], (BATCH, D), 1.0, 6.0, ((1, 8),)),
        "w_query": noise(streams_of[1], (D, HQ * HD), D ** -0.5, 0.046875, ((0, 8), (1, 2))),
        "w_key": noise(streams_of[2], (D, KVH * HD), D ** -0.5, 0.046875, ((0, 8), (1, 2))),
        "w_value": noise(streams_of[3], (D, KVH * HD), D ** -0.5, 0.046875, ((0, 8), (1, 2))),
        "w_out": noise(streams_of[4], (HQ * HD, D), (HQ * HD) ** -0.5, 0.0625, ((0, 2), (1, 8))),
        "key_cache": draw_key_cache(jax.random.fold_in(jax.random.fold_in(streams_of[8], part), 71), part),
        "value_cache": noise(part_keys[6], (BATCH, KVH, CACHE, HD), 1.0, 6.0, ((0, 8), (1, 2))),
        "lengths": draw_lengths(jax.random.fold_in(jax.random.fold_in(streams_of[8], part), 71), part),
    }


rope_base = 500000.0


def rotate(vectors, positions):
    half = vectors.shape[-1] // 2
    freqs = rope_base ** (-2.0 * jnp.arange(half).astype(jnp.float32) / (2.0 * half))
    angles = positions[:, None] * freqs[None, :]
    cosine = jnp.cos(angles)[:, None, :]
    sine = jnp.sin(angles)[:, None, :]
    first = vectors[..., :half]
    second = vectors[..., half:]
    return jnp.concatenate([first * cosine - second * sine, second * cosine + first * sine], axis=-1)


def attend_row(packed):
    queries_rot, keys_rot, values_b, cache_keys, cache_values, length = packed
    scaling = HD ** -0.5
    scores = jnp.einsum("kgd,kcd->kgc", queries_rot.astype(jnp.float32), cache_keys.astype(jnp.float32)) * scaling
    own_score = jnp.einsum("kgd,kd->kg", queries_rot.astype(jnp.float32), keys_rot.astype(jnp.float32)) * scaling
    valid = jnp.arange(CACHE).astype(jnp.int32) < length
    scores = jnp.where(valid[None, None, :], scores, jnp.float32(-1e30))
    highest = jnp.maximum(jnp.max(scores, axis=-1), own_score)
    weights = jnp.exp(scores - highest[..., None])
    own_weight = jnp.exp(own_score - highest)
    total = jnp.sum(weights, axis=-1) + own_weight
    probs = (weights / total[..., None]).astype(jnp.bfloat16)
    own_prob = (own_weight / total).astype(jnp.bfloat16)
    mixed = jnp.einsum("kgc,kcd->kgd", probs.astype(jnp.float32), cache_values.astype(jnp.float32))
    mixed = mixed + own_prob.astype(jnp.float32)[..., None] * values_b.astype(jnp.float32)[:, None, :]
    return mixed.astype(jnp.bfloat16)


def reference(tokens, w_query, w_key, w_value, w_out, key_cache, value_cache, lengths):
    positions = lengths.astype(jnp.float32)
    queries = jnp.dot(tokens, w_query, preferred_element_type=jnp.float32)
    keys_new = jnp.dot(tokens, w_key, preferred_element_type=jnp.float32)
    values_new = jnp.dot(tokens, w_value, preferred_element_type=jnp.float32)
    queries_rot = rotate(queries.reshape(BATCH, HQ, HD), positions).astype(jnp.bfloat16)
    queries_rot = queries_rot.reshape(BATCH, KVH, HQ // KVH, HD)
    keys_rot = rotate(keys_new.reshape(BATCH, KVH, HD), positions).astype(jnp.bfloat16)
    values_b = values_new.astype(jnp.bfloat16).reshape(BATCH, KVH, HD)
    heads = lax.map(attend_row, (queries_rot, keys_rot, values_b, key_cache, value_cache, lengths))
    heads = heads.reshape(BATCH, HQ * HD)
    return jnp.dot(heads, w_out, preferred_element_type=jnp.float32).astype(jnp.bfloat16)
```

```python
import functools

import jax
import jax.numpy as jnp
from jax import lax
from jax.experimental import pallas as pl
from jax.experimental.pallas import tpu as pltpu
from jax.sharding import PartitionSpec as P

rope_base = 500000.0
MIB = 1024 * 1024


def project_kernel(
    n,
    head_dim,
    tokens_ref,
    wq_ref,
    wk_ref,
    wv_ref,
    out_ref,
    t_buf,
    q_buf,
    k_buf,
    v_buf,
    by_head,
    k_rows,
    v_rows,
    sems,
):
    rows = tokens_ref.shape[0]
    chunks, _, width = q_buf.shape
    heads = chunks * width // head_dim
    kv_heads = wk_ref.shape[1] // head_dim
    t_copy = pltpu.make_async_copy(tokens_ref, t_buf, sems.at[2 + chunks])
    k_copy = pltpu.make_async_copy(wk_ref, k_buf, sems.at[0])
    v_copy = pltpu.make_async_copy(wv_ref, v_buf, sems.at[1])
    t_copy.start()
    k_copy.start()
    v_copy.start()
    q_copies = []
    for c in range(chunks):
        copy = pltpu.make_async_copy(
            wq_ref.at[:, c * width : (c + 1) * width], q_buf.at[c], sems.at[2 + c]
        )
        copy.start()
        q_copies.append(copy)
    t_copy.wait()
    tokens = t_buf[...]

    def spread(dest, part, first, count):
        for j in range(part.shape[1] // head_dim):
            dest[pl.ds(first + j, rows, stride=count), :] = part[:, j * head_dim : (j + 1) * head_dim]

    k_copy.wait()
    spread(k_rows, jnp.dot(tokens, k_buf[...], preferred_element_type=jnp.float32), 0, kv_heads)
    v_copy.wait()
    spread(v_rows, jnp.dot(tokens, v_buf[...], preferred_element_type=jnp.float32), 0, kv_heads)
    for c in range(chunks):
        q_copies[c].wait()
        part = jnp.dot(tokens, q_buf[c], preferred_element_type=jnp.float32)
        spread(by_head, part, c * (width // head_dim), heads)
    own = rows // n
    for d in range(n):
        out_ref[d, : own * heads] = by_head[d * own * heads : (d + 1) * own * heads].astype(out_ref.dtype)
        kv = jnp.concatenate(
            [
                k_rows[d * own * kv_heads : (d + 1) * own * kv_heads],
                v_rows[d * own * kv_heads : (d + 1) * own * kv_heads],
            ],
            axis=0,
        )
        out_ref[d, own * heads :] = kv.astype(out_ref.dtype)


def attend_kernel(n, lengths_ref, parts_ref, cos_ref, sin_ref, key_ref, value_ref, out_ref, keys, values, sems):
    rows, kv_heads, slots, head_dim = key_ref.shape
    heads = out_ref.shape[1] // rows
    group = heads // kv_heads
    pairs = [(r, k) for r in range(rows) for k in range(kv_heads)]
    copies = {}
    for i, (r, k) in enumerate(pairs):
        copies["k", i] = pltpu.make_async_copy(key_ref.at[r, k], keys.at[i], sems.at[0, i])
        copies["k", i].start()
    for i, (r, k) in enumerate(pairs):
        copies["v", i] = pltpu.make_async_copy(value_ref.at[r, k], values.at[i], sems.at[1, i])
        copies["v", i].start()

    total = parts_ref[0].astype(jnp.float32)
    for d in range(1, n):
        total = total + parts_ref[d].astype(jnp.float32)
    cosine = cos_ref[...]
    sine = sin_ref[...]

    def rotated(vectors, count):
        per_row = (rows, count, head_dim)
        c = jnp.broadcast_to(cosine[:, None, :], per_row).reshape(rows * count, head_dim)
        s = jnp.broadcast_to(sine[:, None, :], per_row).reshape(rows * count, head_dim)
        return (vectors * c + pltpu.roll(vectors, head_dim // 2, 1) * s).astype(jnp.bfloat16)

    q_count = rows * heads
    kv_count = rows * kv_heads
    queries = rotated(total[:q_count], heads)
    new_keys = rotated(total[q_count : q_count + kv_count], kv_heads).astype(jnp.float32)
    new_values = total[q_count + kv_count :].astype(jnp.bfloat16).astype(jnp.float32)
    scaling = head_dim ** (-0.5)
    slot = lax.broadcasted_iota(jnp.int32, (group, slots), 1)
    scores = []
    own_scores = []
    for i, (r, k) in enumerate(pairs):
        q = queries[i * group : (i + 1) * group]
        copies["k", i].wait()
        score = lax.dot_general(
            q, keys[i], (((1,), (1,)), ((), ())), preferred_element_type=jnp.float32
        )
        scores.append(jnp.where(slot < lengths_ref[r], score * scaling, jnp.float32(-1e30)))
        own_scores.append(
            jnp.sum(q.astype(jnp.float32) * new_keys[i : i + 1], axis=1, keepdims=True) * scaling
        )
    highest = [
        jnp.maximum(jnp.max(score, axis=1, keepdims=True), own)
        for score, own in zip(scores, own_scores)
    ]
    weights = [jnp.exp(score - high) for score, high in zip(scores, highest)]
    own_weights = [jnp.exp(own - high) for own, high in zip(own_scores, highest)]
    norms = [
        jnp.sum(weight, axis=1, keepdims=True) + own for weight, own in zip(weights, own_weights)
    ]
    mixed = []
    for i in range(len(pairs)):
        copies["v", i].wait()
        head = jnp.dot(weights[i].astype(jnp.bfloat16), values[i], preferred_element_type=jnp.float32)
        mixed.append((head + own_weights[i] * new_values[i : i + 1]) / norms[i])
    block = jnp.concatenate(mixed, axis=0).astype(jnp.bfloat16)
    for d in range(n):
        out_ref[d] = block


def output_kernel(n, gy, me_ref, heads_ref, w_ref, own_ref, other_ref, w_buf, wide, lhs, sems):
    chunks, _, width = w_buf.shape
    copies = []
    for c in range(chunks):
        copy = pltpu.make_async_copy(
            w_ref.at[:, c * width : (c + 1) * width], w_buf.at[c], sems.at[c]
        )
        copy.start()
        copies.append(copy)
    own = n // gy
    per_dev, head_dim = heads_ref.shape[1:]
    heads = w_ref.shape[0] // head_dim
    rows = n * per_dev // heads
    for j in range(gy):
        first = lax.rem(me_ref[0] + j, gy) * own
        for d in range(own):
            at = (j * own + d) * per_dev
            wide[at : at + per_dev, :] = heads_ref[first + d].astype(jnp.float32)
    for h in range(heads):
        lhs[:, h * head_dim : (h + 1) * head_dim] = wide[pl.ds(h, rows, stride=heads), :].astype(lhs.dtype)
    for c in range(chunks):
        copies[c].wait()
        part = jnp.dot(lhs[...], w_buf[c], preferred_element_type=jnp.float32)
        own_ref[:, c * width : (c + 1) * width] = part[: rows // gy]
        for j in range(1, gy):
            other_ref[j - 1, :, c * width : (c + 1) * width] = part[j * (rows // gy) : (j + 1) * (rows // gy)]


def in_hbm(x):
    return pltpu.with_memory_space_constraint(x, pltpu.HBM)


def on_device(n, gy, tokens, w_query, w_key, w_value, w_out, key_cache, value_cache, lengths):
    own_rows, kv_heads, slots, head_dim = key_cache.shape
    rows, depth = tokens.shape
    q_cols = w_query.shape[1]
    kv_cols = w_key.shape[1]
    heads = q_cols // head_dim
    out_cols = w_out.shape[1]
    vmem = pl.BlockSpec(memory_space=pltpu.VMEM)
    smem = pl.BlockSpec(memory_space=pltpu.SMEM)
    anywhere = pl.BlockSpec(memory_space=pl.ANY)
    width = min(512, q_cols)
    chunks = q_cols // width
    block = own_rows * (heads + 2 * kv_heads)

    parts = pl.pallas_call(
        functools.partial(project_kernel, n, head_dim),
        out_shape=jax.ShapeDtypeStruct((n, block, head_dim), jnp.bfloat16),
        in_specs=[anywhere, anywhere, anywhere, anywhere],
        out_specs=vmem,
        scratch_shapes=[
            pltpu.VMEM((rows, depth), jnp.bfloat16),
            pltpu.VMEM((chunks, depth, width), jnp.bfloat16),
            pltpu.VMEM((depth, kv_cols), jnp.bfloat16),
            pltpu.VMEM((depth, kv_cols), jnp.bfloat16),
            pltpu.VMEM((rows * heads, head_dim), jnp.float32),
            pltpu.VMEM((rows * kv_heads, head_dim), jnp.float32),
            pltpu.VMEM((rows * kv_heads, head_dim), jnp.float32),
            pltpu.SemaphoreType.DMA((3 + chunks,)),
        ],
        compiler_params=pltpu.CompilerParams(vmem_limit_bytes=26 * MIB),
        cost_estimate=pl.CostEstimate(
            flops=2 * rows * depth * (q_cols + 2 * kv_cols),
            bytes_accessed=2 * depth * (q_cols + 2 * kv_cols),
            transcendentals=0,
        ),
        name="project",
    )(in_hbm(tokens), in_hbm(w_query), in_hbm(w_key), in_hbm(w_value))

    parts = lax.all_to_all(parts, "gx", 0, 0, tiled=True)

    half = head_dim // 2
    freqs = rope_base ** (-2.0 * jnp.arange(half).astype(jnp.float32) / (2.0 * half))
    angles = lengths.astype(jnp.float32)[:, None] * freqs[None, :]
    cosine = jnp.cos(angles)
    sine = jnp.sin(angles)
    cosine = jnp.concatenate([cosine, cosine], axis=1)
    sine = jnp.concatenate([-sine, sine], axis=1)

    mixed = pl.pallas_call(
        functools.partial(attend_kernel, n),
        out_shape=jax.ShapeDtypeStruct((n, own_rows * heads, head_dim), jnp.bfloat16),
        in_specs=[smem, vmem, vmem, vmem, anywhere, anywhere],
        out_specs=vmem,
        scratch_shapes=[
            pltpu.VMEM((own_rows * kv_heads, slots, head_dim), jnp.bfloat16),
            pltpu.VMEM((own_rows * kv_heads, slots, head_dim), jnp.bfloat16),
            pltpu.SemaphoreType.DMA((2, own_rows * kv_heads)),
        ],
        compiler_params=pltpu.CompilerParams(vmem_limit_bytes=16 * MIB),
        cost_estimate=pl.CostEstimate(
            flops=4 * own_rows * heads * slots * head_dim,
            bytes_accessed=4 * own_rows * kv_heads * slots * head_dim,
            transcendentals=own_rows * heads * slots,
        ),
        name="attend",
    )(
        lengths,
        parts,
        cosine,
        sine,
        in_hbm(key_cache),
        in_hbm(value_cache),
    )

    mixed = lax.all_to_all(mixed, "gx", 0, 0, tiled=True)

    me = lax.axis_index("gy").astype(jnp.int32).reshape(1)
    out_width = min(256, out_cols)
    out_chunks = out_cols // out_width
    own, other = pl.pallas_call(
        functools.partial(output_kernel, n, gy),
        out_shape=(
            jax.ShapeDtypeStruct((rows // gy, out_cols), jnp.float32),
            jax.ShapeDtypeStruct((gy - 1, rows // gy, out_cols), jnp.float32),
        ),
        in_specs=[smem, vmem, anywhere],
        out_specs=(vmem, vmem),
        scratch_shapes=[
            pltpu.VMEM((out_chunks, q_cols, out_width), jnp.bfloat16),
            pltpu.VMEM((rows * heads, head_dim), jnp.float32),
            pltpu.VMEM((rows, q_cols), jnp.bfloat16),
            pltpu.SemaphoreType.DMA((out_chunks,)),
        ],
        compiler_params=pltpu.CompilerParams(vmem_limit_bytes=26 * MIB),
        cost_estimate=pl.CostEstimate(
            flops=2 * rows * q_cols * out_cols,
            bytes_accessed=2 * q_cols * out_cols,
            transcendentals=0,
        ),
        name="output",
    )(me, mixed, in_hbm(w_out))

    total = own
    for j in range(1, gy):
        total = total + lax.ppermute(other[j - 1], "gy", [(i, (i + j) % gy) for i in range(gy)])
    return total.astype(jnp.bfloat16)


def solution(mesh):
    in_specs = (
        P("groups", "gx"),
        P("gx", "gy"),
        P("gx", "gy"),
        P("gx", "gy"),
        P("gy", "gx"),
        P(("groups", "gx"), "gy", None, None),
        P(("groups", "gx"), "gy", None, None),
        P(("groups", "gx")),
    )
    out_specs = P(("groups", "gy"), "gx")
    body = functools.partial(on_device, mesh.shape["gx"], mesh.shape["gy"])
    return jax.shard_map(body, mesh=mesh, in_specs=in_specs, out_specs=out_specs, check_vma=False)
```

```python
import functools

import jax
import jax.numpy as jnp
from jax import lax
from jax.experimental import pallas as pl
from jax.experimental.pallas import tpu as pltpu
from jax.sharding import PartitionSpec as P

rope_base = 500000.0
MIB = 1024 * 1024


def project_kernel(
    head_dim,
    me_ref,
    tokens_ref,
    wq_ref,
    wk_ref,
    wv_ref,
    keep_ref,
    send_ref,
    t_buf,
    q_buf,
    k_buf,
    v_buf,
    by_head,
    k_rows,
    v_rows,
    sems,
):
    rows = tokens_ref.shape[0]
    chunks, _, width = q_buf.shape
    heads = chunks * width // head_dim
    kv_heads = wk_ref.shape[1] // head_dim
    t_copy = pltpu.make_async_copy(tokens_ref, t_buf, sems.at[2 + chunks])
    k_copy = pltpu.make_async_copy(wk_ref, k_buf, sems.at[0])
    v_copy = pltpu.make_async_copy(wv_ref, v_buf, sems.at[1])
    t_copy.start()
    k_copy.start()
    v_copy.start()
    q_copies = []
    for c in range(chunks):
        copy = pltpu.make_async_copy(
            wq_ref.at[:, c * width : (c + 1) * width], q_buf.at[c], sems.at[2 + c]
        )
        copy.start()
        q_copies.append(copy)
    t_copy.wait()
    tokens = t_buf[...]

    def spread(dest, part, first, count):
        for j in range(part.shape[1] // head_dim):
            dest[pl.ds(first + j, rows, stride=count), :] = part[:, j * head_dim : (j + 1) * head_dim]

    k_copy.wait()
    spread(k_rows, jnp.dot(tokens, k_buf[...], preferred_element_type=jnp.float32), 0, kv_heads)
    v_copy.wait()
    spread(v_rows, jnp.dot(tokens, v_buf[...], preferred_element_type=jnp.float32), 0, kv_heads)
    for c in range(chunks):
        q_copies[c].wait()
        part = jnp.dot(tokens, q_buf[c], preferred_element_type=jnp.float32)
        spread(by_head, part, c * (width // head_dim), heads)
    far, block, _ = keep_ref.shape
    near = rows * (heads + 2 * kv_heads) // (far * block)
    own = rows // (far * near)

    def of_device(d):
        def pick(source, count):
            size = own * count
            return source[pl.ds(pl.multiple_of(d * size, size), size), :]

        return jnp.concatenate([pick(by_head, heads), pick(k_rows, kv_heads), pick(v_rows, kv_heads)], axis=0)

    mine = lax.rem(me_ref[0], near)
    for f in range(far):
        keep_ref[f] = of_device(f * near + mine)
        for j in range(1, near):
            send_ref[j - 1, f] = of_device(f * near + lax.rem(mine + j, near)).astype(send_ref.dtype)


def partner(f, k, far):
    return f ^ k if far & (far - 1) == 0 else (f + k) % far


def source(f, k, far):
    return f ^ k if far & (far - 1) == 0 else (f + far - k) % far


def combine_kernel(near, me_ref, cache_ref, keep_ref, *refs):
    far = keep_ref.shape[0]
    mine = lax.div(me_ref[0], near)
    received, outs = refs[:-far], refs[-far:]
    for k in range(far):
        f = partner(mine, k, far)
        total = keep_ref[f]
        for part in received:
            total = total + part[f].astype(jnp.float32)
        outs[k][...] = total.astype(outs[k].dtype)


def attend_kernel(lengths_ref, cos_ref, sin_ref, keys, values, *refs):
    parts, out_ref = refs[:-1], refs[-1]
    rows, kv_heads, slots, head_dim = keys.shape
    heads = out_ref.shape[0] // rows
    group = heads // kv_heads
    pairs = [(r, k) for r in range(rows) for k in range(kv_heads)]
    total = parts[0][...].astype(jnp.float32)
    for part in parts[1:]:
        total = total + part[...].astype(jnp.float32)
    cosine = cos_ref[...]
    sine = sin_ref[...]

    def rotated(vectors, count):
        per_row = (rows, count, head_dim)
        c = jnp.broadcast_to(cosine[:, None, :], per_row).reshape(rows * count, head_dim)
        s = jnp.broadcast_to(sine[:, None, :], per_row).reshape(rows * count, head_dim)
        return (vectors * c + pltpu.roll(vectors, head_dim // 2, 1) * s).astype(jnp.bfloat16)

    q_count = rows * heads
    kv_count = rows * kv_heads
    queries = rotated(total[:q_count], heads)
    new_keys = rotated(total[q_count : q_count + kv_count], kv_heads).astype(jnp.float32)
    new_values = total[q_count + kv_count :].astype(jnp.bfloat16).astype(jnp.float32)
    scaling = head_dim ** (-0.5)
    slot = lax.broadcasted_iota(jnp.int32, (group, slots), 1)
    scores = []
    own_scores = []
    for i, (r, k) in enumerate(pairs):
        q = queries[i * group : (i + 1) * group]
        score = lax.dot_general(
            q, keys[r, k], (((1,), (1,)), ((), ())), preferred_element_type=jnp.float32
        )
        scores.append(jnp.where(slot < lengths_ref[r], score * scaling, jnp.float32(-1e30)))
        own_scores.append(
            jnp.sum(q.astype(jnp.float32) * new_keys[i : i + 1], axis=1, keepdims=True) * scaling
        )
    highest = [
        jnp.maximum(jnp.max(score, axis=1, keepdims=True), own)
        for score, own in zip(scores, own_scores)
    ]
    weights = [jnp.exp(score - high) for score, high in zip(scores, highest)]
    own_weights = [jnp.exp(own - high) for own, high in zip(own_scores, highest)]
    norms = [
        jnp.sum(weight, axis=1, keepdims=True) + own for weight, own in zip(weights, own_weights)
    ]
    mixed = []
    for i, (r, k) in enumerate(pairs):
        head = jnp.dot(weights[i].astype(jnp.bfloat16), values[r, k], preferred_element_type=jnp.float32)
        mixed.append((head + own_weights[i] * new_values[i : i + 1]) / norms[i])
    out_ref[...] = jnp.concatenate(mixed, axis=0).astype(jnp.bfloat16)


def output_kernel(n, gy, far, me_ref, w_ref, *refs):
    blocks = refs[:far]
    own_ref, other_ref, wide, lhs = refs[far:]
    near, per_dev, head_dim = blocks[0].shape
    heads = w_ref.shape[0] // head_dim
    rows = n * per_dev // heads
    out_cols = w_ref.shape[1]
    width = min(512, out_cols)
    half = n // gy
    mine = lax.rem(me_ref[0], near)
    for k in range(far):
        for j in range(near):
            d = source(lax.div(me_ref[0], near), k, far) * near + lax.rem(mine + near - j, near)
            place = lax.rem(lax.div(d, half) + gy - me_ref[1], gy) * half + lax.rem(d, half)
            wide[pl.ds(pl.multiple_of(place * per_dev, per_dev), per_dev), :] = blocks[k][j].astype(jnp.float32)
    for h in range(heads):
        lhs[:, h * head_dim : (h + 1) * head_dim] = wide[pl.ds(h, rows, stride=heads), :].astype(lhs.dtype)
    for c in range(out_cols // width):
        part = jnp.dot(
            lhs[...], w_ref[:, c * width : (c + 1) * width], preferred_element_type=jnp.float32
        )
        own_ref[:, c * width : (c + 1) * width] = part[: rows // gy]
        for j in range(1, gy):
            other_ref[j - 1, :, c * width : (c + 1) * width] = part[j * (rows // gy) : (j + 1) * (rows // gy)]


def in_hbm(x):
    return pltpu.with_memory_space_constraint(x, pltpu.HBM)


def in_vmem(x):
    return pltpu.with_memory_space_constraint(x, pltpu.VMEM)


def on_device(n, gy, tokens, w_query, w_key, w_value, w_out, key_cache, value_cache, lengths):
    own_rows, kv_heads, slots, head_dim = key_cache.shape
    rows, depth = tokens.shape
    q_cols = w_query.shape[1]
    kv_cols = w_key.shape[1]
    heads = q_cols // head_dim
    out_cols = w_out.shape[1]
    vmem = pl.BlockSpec(memory_space=pltpu.VMEM)
    smem = pl.BlockSpec(memory_space=pltpu.SMEM)
    anywhere = pl.BlockSpec(memory_space=pl.ANY)
    width = min(512, q_cols)
    chunks = q_cols // width
    block = own_rows * (heads + 2 * kv_heads)

    near = 2 if n % 2 == 0 else 1
    far = n // near
    def to_near(x, j):
        return lax.ppermute(
            x, "gx", [(f * near + i, f * near + (i + j) % near) for f in range(far) for i in range(near)]
        )

    def to_far(x, k):
        return lax.ppermute(
            x, "gx", [(f * near + i, int(partner(f, k, far)) * near + i) for f in range(far) for i in range(near)]
        )

    me = jnp.stack([lax.axis_index("gx"), lax.axis_index("gy")]).astype(jnp.int32)

    keep, send = pl.pallas_call(
        functools.partial(project_kernel, head_dim),
        out_shape=(
            jax.ShapeDtypeStruct((far, block, head_dim), jnp.float32),
            jax.ShapeDtypeStruct((near - 1, far, block, head_dim), jnp.bfloat16),
        ),
        in_specs=[smem, anywhere, anywhere, anywhere, anywhere],
        out_specs=(vmem, vmem),
        scratch_shapes=[
            pltpu.VMEM((rows, depth), jnp.bfloat16),
            pltpu.VMEM((chunks, depth, width), jnp.bfloat16),
            pltpu.VMEM((depth, kv_cols), jnp.bfloat16),
            pltpu.VMEM((depth, kv_cols), jnp.bfloat16),
            pltpu.VMEM((rows * heads, head_dim), jnp.float32),
            pltpu.VMEM((rows * kv_heads, head_dim), jnp.float32),
            pltpu.VMEM((rows * kv_heads, head_dim), jnp.float32),
            pltpu.SemaphoreType.DMA((3 + chunks,)),
        ],
        compiler_params=pltpu.CompilerParams(vmem_limit_bytes=26 * MIB),
        cost_estimate=pl.CostEstimate(
            flops=2 * rows * depth * (q_cols + 2 * kv_cols),
            bytes_accessed=2 * depth * (q_cols + 2 * kv_cols),
            transcendentals=0,
        ),
        name="project",
    )(me, in_hbm(tokens), in_hbm(w_query), in_hbm(w_key), in_hbm(w_value))

    received = [to_near(send[j - 1], j) for j in range(1, near)]

    summed = pl.pallas_call(
        functools.partial(combine_kernel, near),
        out_shape=[
            jax.ShapeDtypeStruct((block, head_dim), jnp.float32 if k == 0 else jnp.bfloat16)
            for k in range(far)
        ],
        in_specs=[smem] + [vmem] * (2 + len(received)),
        out_specs=[vmem] * far,
        compiler_params=pltpu.CompilerParams(vmem_limit_bytes=12 * MIB),
        cost_estimate=pl.CostEstimate(flops=0, bytes_accessed=16 * MIB, transcendentals=0),
        name="combine",
    )(me, in_vmem(value_cache), keep, *received)

    parts = [summed[0]] + [to_far(summed[k], k) for k in range(1, far)]

    half = head_dim // 2
    freqs = rope_base ** (-2.0 * jnp.arange(half).astype(jnp.float32) / (2.0 * half))
    angles = lengths.astype(jnp.float32)[:, None] * freqs[None, :]
    cosine = jnp.cos(angles)
    sine = jnp.sin(angles)
    cosine = jnp.concatenate([cosine, cosine], axis=1)
    sine = jnp.concatenate([-sine, sine], axis=1)

    mixed = pl.pallas_call(
        attend_kernel,
        out_shape=jax.ShapeDtypeStruct((own_rows * heads, head_dim), jnp.bfloat16),
        in_specs=[smem] + [vmem] * (4 + far),
        out_specs=vmem,
        compiler_params=pltpu.CompilerParams(vmem_limit_bytes=12 * MIB),
        cost_estimate=pl.CostEstimate(
            flops=4 * own_rows * heads * slots * head_dim,
            bytes_accessed=4 * own_rows * kv_heads * slots * head_dim,
            transcendentals=own_rows * heads * slots,
        ),
        name="attend",
    )(lengths, cosine, sine, in_vmem(key_cache), in_vmem(value_cache), *parts)

    pair = jnp.stack([mixed] + [to_near(mixed, j) for j in range(1, near)])
    blocks = [pair] + [to_far(pair, k) for k in range(1, far)]

    own, other = pl.pallas_call(
        functools.partial(output_kernel, n, gy, far),
        out_shape=(
            jax.ShapeDtypeStruct((rows // gy, out_cols), jnp.float32),
            jax.ShapeDtypeStruct((gy - 1, rows // gy, out_cols), jnp.float32),
        ),
        in_specs=[smem] + [vmem] * (1 + far),
        out_specs=(vmem, vmem),
        scratch_shapes=[
            pltpu.VMEM((rows * heads, head_dim), jnp.float32),
            pltpu.VMEM((rows, q_cols), jnp.bfloat16),
        ],
        compiler_params=pltpu.CompilerParams(vmem_limit_bytes=12 * MIB),
        cost_estimate=pl.CostEstimate(
            flops=2 * rows * q_cols * out_cols,
            bytes_accessed=2 * q_cols * out_cols,
            transcendentals=0,
        ),
        name="output",
    )(me, in_vmem(w_out), *blocks)

    total = own
    for j in range(1, gy):
        total = total + lax.ppermute(other[j - 1], "gy", [(i, (i + j) % gy) for i in range(gy)])
    return total.astype(jnp.bfloat16)


def solution(mesh):
    in_specs = (
        P("groups", "gx"),
        P("gx", "gy"),
        P("gx", "gy"),
        P("gx", "gy"),
        P("gy", "gx"),
        P(("groups", "gx"), "gy", None, None),
        P(("groups", "gx"), "gy", None, None),
        P(("groups", "gx")),
    )
    out_specs = P(("groups", "gy"), "gx")
    body = functools.partial(on_device, mesh.shape["gx"], mesh.shape["gy"])
    return jax.shard_map(body, mesh=mesh, in_specs=in_specs, out_specs=out_specs, check_vma=False)
```

```python
import functools

import jax
import jax.numpy as jnp
from jax import lax
from jax.experimental import pallas as pl
from jax.experimental.pallas import tpu as pltpu
from jax.sharding import PartitionSpec as P

rope_base = 500000.0
MIB = 1024 * 1024


def chunk_widths(cols, head_dim):
    unit = cols // 16
    if cols % 16 or unit % head_dim:
        return (cols,)
    return (4 * unit, 4 * unit, 4 * unit, 2 * unit, unit, unit)


def project_kernel(
    near,
    widths,
    head_dim,
    tokens_ref,
    wq_ref,
    wk_ref,
    wv_ref,
    keep_ref,
    send_ref,
    t_buf,
    q_buf,
    k_buf,
    v_buf,
    by_head,
    k_rows,
    v_rows,
    sems,
):
    rows = tokens_ref.shape[0]
    heads = q_buf.shape[1] // head_dim
    kv_heads = wk_ref.shape[1] // head_dim
    t_copy = pltpu.make_async_copy(tokens_ref, t_buf, sems.at[0])
    k_copy = pltpu.make_async_copy(wk_ref, k_buf, sems.at[1])
    v_copy = pltpu.make_async_copy(wv_ref, v_buf, sems.at[2])
    t_copy.start()
    k_copy.start()
    v_copy.start()
    q_copies = []
    first = 0
    for c, width in enumerate(widths):
        at = slice(first, first + width)
        copy = pltpu.make_async_copy(wq_ref.at[:, at], q_buf.at[:, at], sems.at[3 + c])
        copy.start()
        q_copies.append((copy, at))
        first += width

    far, block, _ = keep_ref.shape
    own = rows // (far * near)
    q_count = own * heads
    me = lax.axis_index("gx")
    mine, mine_far = lax.rem(me, near), lax.div(me, near)

    def devices():
        for f in range(far):
            other = partner(mine_far, f, far) * near
            yield keep_ref, (f,), other + mine
            for j in range(1, near):
                yield send_ref, (j - 1, f), other + lax.rem(mine + j, near)

    def spread(dest, part, first, count):
        for j in range(part.shape[1] // head_dim):
            dest[pl.ds(first + j, rows, stride=count), :] = part[:, j * head_dim : (j + 1) * head_dim]

    def put_kv():
        for ref, at, d in devices():
            size = own * kv_heads
            rows_of = pl.ds(pl.multiple_of(d * size, size), size)
            kv = jnp.concatenate([k_rows[rows_of, :], v_rows[rows_of, :]], axis=0)
            ref[*at, q_count:, :] = kv.astype(ref.dtype)

    def put_heads(first, count):
        for ref, at, d in devices():
            start = pl.multiple_of(d * q_count, q_count)
            for r in range(own):
                to = r * heads + first
                ref[*at, to : to + count, :] = by_head[pl.ds(start + to, count), :].astype(ref.dtype)

    t_copy.wait()
    tokens = t_buf[...]
    k_copy.wait()
    spread(k_rows, jnp.dot(tokens, k_buf[...], preferred_element_type=jnp.float32), 0, kv_heads)
    v_copy.wait()
    spread(v_rows, jnp.dot(tokens, v_buf[...], preferred_element_type=jnp.float32), 0, kv_heads)
    put_kv()
    step = 16 if heads % 16 == 0 else heads
    done = 0
    for copy, at in q_copies:
        copy.wait()
        part = jnp.dot(tokens, q_buf[:, at], preferred_element_type=jnp.float32)
        spread(by_head, part, at.start // head_dim, heads)
        while done + step <= at.stop // head_dim:
            put_heads(done, step)
            done += step


def partner(f, k, far):
    return f ^ k if far & (far - 1) == 0 else (f + k) % far


def source(f, k, far):
    return f ^ k if far & (far - 1) == 0 else (f + far - k) % far


def combine_kernel(cache_ref, keep_ref, *refs):
    far = keep_ref.shape[0]
    received, outs = refs[:-far], refs[-far:]
    for k in range(far):
        total = keep_ref[k]
        for part in received:
            total = total + part[k].astype(jnp.float32)
        outs[k][...] = total.astype(outs[k].dtype)


def attend_kernel(table_ref, keys, values, *refs):
    parts, out_ref = refs[:-1], refs[-1]
    rows, kv_heads, slots, head_dim = keys.shape
    heads = out_ref.shape[0] // rows
    group = heads // kv_heads
    pairs = [(r, k) for r in range(rows) for k in range(kv_heads)]
    total = parts[0][...].astype(jnp.float32)
    for part in parts[1:]:
        total = total + part[...].astype(jnp.float32)
    cosine = table_ref[:rows]
    sine = table_ref[rows : 2 * rows]
    filled = table_ref[2 * rows :]

    def rotated(vectors, count):
        per_row = (rows, count, head_dim)
        c = jnp.broadcast_to(cosine[:, None, :], per_row).reshape(rows * count, head_dim)
        s = jnp.broadcast_to(sine[:, None, :], per_row).reshape(rows * count, head_dim)
        return (vectors * c + pltpu.roll(vectors, head_dim // 2, 1) * s).astype(jnp.bfloat16)

    q_count = rows * heads
    kv_count = rows * kv_heads
    queries = rotated(total[:q_count], heads)
    new_keys = rotated(total[q_count : q_count + kv_count], kv_heads).astype(jnp.float32)
    new_values = total[q_count + kv_count :].astype(jnp.bfloat16).astype(jnp.float32)
    scaling = head_dim ** (-0.5)
    slot = lax.broadcasted_iota(jnp.int32, (group, slots), 1).astype(jnp.float32)
    scores = []
    own_scores = []
    for i, (r, k) in enumerate(pairs):
        q = queries[i * group : (i + 1) * group]
        score = lax.dot_general(
            q, keys[r, k], (((1,), (1,)), ((), ())), preferred_element_type=jnp.float32
        )
        scores.append(jnp.where(slot < filled[r : r + 1, :1], score * scaling, jnp.float32(-1e30)))
        own_scores.append(
            jnp.sum(q.astype(jnp.float32) * new_keys[i : i + 1], axis=1, keepdims=True) * scaling
        )
    highest = [
        jnp.maximum(jnp.max(score, axis=1, keepdims=True), own)
        for score, own in zip(scores, own_scores)
    ]
    weights = [jnp.exp(score - high) for score, high in zip(scores, highest)]
    own_weights = [jnp.exp(own - high) for own, high in zip(own_scores, highest)]
    norms = [
        jnp.sum(weight, axis=1, keepdims=True) + own for weight, own in zip(weights, own_weights)
    ]
    mixed = []
    for i, (r, k) in enumerate(pairs):
        head = jnp.dot(weights[i].astype(jnp.bfloat16), values[r, k], preferred_element_type=jnp.float32)
        mixed.append((head + own_weights[i] * new_values[i : i + 1]) / norms[i])
    out_ref[...] = jnp.concatenate(mixed, axis=0).astype(jnp.bfloat16)


def output_kernel(n, gy, far, w_ref, *refs):
    blocks = refs[:far]
    own_ref, other_ref, wide, lhs = refs[far:]
    near, per_dev, head_dim = blocks[0].shape
    heads = w_ref.shape[0] // head_dim
    rows = n * per_dev // heads
    out_cols = w_ref.shape[1]
    width = min(512, out_cols)
    half = n // gy
    me, me_gy = lax.axis_index("gx"), lax.axis_index("gy")
    mine, mine_far = lax.rem(me, near), lax.div(me, near)
    for k in range(far):
        for j in range(near):
            d = source(mine_far, k, far) * near + lax.rem(mine + near - j, near)
            place = lax.rem(lax.div(d, half) + gy - me_gy, gy) * half + lax.rem(d, half)
            wide[pl.ds(pl.multiple_of(place * per_dev, per_dev), per_dev), :] = blocks[k][j].astype(jnp.float32)
    for h in range(heads):
        lhs[:, h * head_dim : (h + 1) * head_dim] = wide[pl.ds(h, rows, stride=heads), :].astype(lhs.dtype)
    for c in range(out_cols // width):
        part = jnp.dot(
            lhs[...], w_ref[:, c * width : (c + 1) * width], preferred_element_type=jnp.float32
        )
        own_ref[:, c * width : (c + 1) * width] = part[: rows // gy]
        for j in range(1, gy):
            other = part[j * (rows // gy) : (j + 1) * (rows // gy)]
            other_ref[j - 1, :, c * width : (c + 1) * width] = other.astype(other_ref.dtype)


def in_hbm(x):
    return pltpu.with_memory_space_constraint(x, pltpu.HBM)


def in_vmem(x):
    return pltpu.with_memory_space_constraint(x, pltpu.VMEM)


def on_device(n, gy, tokens, w_query, w_key, w_value, w_out, key_cache, value_cache, lengths):
    own_rows, kv_heads, slots, head_dim = key_cache.shape
    rows, depth = tokens.shape
    q_cols = w_query.shape[1]
    kv_cols = w_key.shape[1]
    heads = q_cols // head_dim
    out_cols = w_out.shape[1]
    vmem = pl.BlockSpec(memory_space=pltpu.VMEM)
    anywhere = pl.BlockSpec(memory_space=pl.ANY)
    block = own_rows * (heads + 2 * kv_heads)

    near = 2 if n % 2 == 0 else 1
    far = n // near
    def to_near(x, j):
        return lax.ppermute(
            x, "gx", [(f * near + i, f * near + (i + j) % near) for f in range(far) for i in range(near)]
        )

    def to_far(x, k):
        return lax.ppermute(
            x, "gx", [(f * near + i, int(partner(f, k, far)) * near + i) for f in range(far) for i in range(near)]
        )

    widths = chunk_widths(q_cols, head_dim)
    keep, send = pl.pallas_call(
        functools.partial(project_kernel, near, widths, head_dim),
        out_shape=(
            jax.ShapeDtypeStruct((far, block, head_dim), jnp.float32),
            jax.ShapeDtypeStruct((near - 1, far, block, head_dim), jnp.bfloat16),
        ),
        in_specs=[anywhere, anywhere, anywhere, anywhere],
        out_specs=(vmem, vmem),
        scratch_shapes=[
            pltpu.VMEM((rows, depth), jnp.bfloat16),
            pltpu.VMEM((depth, q_cols), jnp.bfloat16),
            pltpu.VMEM((depth, kv_cols), jnp.bfloat16),
            pltpu.VMEM((depth, kv_cols), jnp.bfloat16),
            pltpu.VMEM((rows * heads, head_dim), jnp.float32),
            pltpu.VMEM((rows * kv_heads, head_dim), jnp.float32),
            pltpu.VMEM((rows * kv_heads, head_dim), jnp.float32),
            pltpu.SemaphoreType.DMA((3 + len(widths),)),
        ],
        compiler_params=pltpu.CompilerParams(vmem_limit_bytes=26 * MIB),
        cost_estimate=pl.CostEstimate(
            flops=2 * rows * depth * (q_cols + 2 * kv_cols),
            bytes_accessed=2 * depth * (q_cols + 2 * kv_cols),
            transcendentals=0,
        ),
        name="project",
    )(in_hbm(tokens), in_hbm(w_query), in_hbm(w_key), in_hbm(w_value))

    received = [to_near(send[j - 1], j) for j in range(1, near)]

    summed = pl.pallas_call(
        combine_kernel,
        out_shape=[
            jax.ShapeDtypeStruct((block, head_dim), jnp.float32 if k == 0 else jnp.bfloat16)
            for k in range(far)
        ],
        in_specs=[vmem] * (2 + len(received)),
        out_specs=[vmem] * far,
        compiler_params=pltpu.CompilerParams(vmem_limit_bytes=12 * MIB),
        cost_estimate=pl.CostEstimate(flops=0, bytes_accessed=16 * MIB, transcendentals=0),
        name="combine",
    )(in_vmem(value_cache), keep, *received)

    parts = [summed[0]] + [to_far(summed[k], k) for k in range(1, far)]

    half = head_dim // 2
    freqs = rope_base ** (-2.0 * jnp.arange(half).astype(jnp.float32) / (2.0 * half))
    positions = lengths.astype(jnp.float32)[:, None]
    angles = positions * freqs[None, :]
    cosine = jnp.cos(angles)
    sine = jnp.sin(angles)
    table = jnp.concatenate(
        [
            jnp.concatenate([cosine, cosine], axis=1),
            jnp.concatenate([-sine, sine], axis=1),
            jnp.broadcast_to(positions, (own_rows, head_dim)),
        ],
        axis=0,
    )

    mixed = pl.pallas_call(
        attend_kernel,
        out_shape=jax.ShapeDtypeStruct((own_rows * heads, head_dim), jnp.bfloat16),
        in_specs=[vmem] * (3 + far),
        out_specs=vmem,
        compiler_params=pltpu.CompilerParams(vmem_limit_bytes=12 * MIB),
        cost_estimate=pl.CostEstimate(
            flops=4 * own_rows * heads * slots * head_dim,
            bytes_accessed=4 * own_rows * kv_heads * slots * head_dim,
            transcendentals=own_rows * heads * slots,
        ),
        name="attend",
    )(table, in_vmem(key_cache), in_vmem(value_cache), *parts)

    pair = jnp.stack([mixed] + [to_near(mixed, j) for j in range(1, near)])
    blocks = [pair] + [to_far(pair, k) for k in range(1, far)]

    own, other = pl.pallas_call(
        functools.partial(output_kernel, n, gy, far),
        out_shape=(
            jax.ShapeDtypeStruct((rows // gy, out_cols), jnp.float32),
            jax.ShapeDtypeStruct((gy - 1, rows // gy, out_cols), jnp.bfloat16),
        ),
        in_specs=[vmem] * (1 + far),
        out_specs=(vmem, vmem),
        scratch_shapes=[
            pltpu.VMEM((rows * heads, head_dim), jnp.float32),
            pltpu.VMEM((rows, q_cols), jnp.bfloat16),
        ],
        compiler_params=pltpu.CompilerParams(vmem_limit_bytes=12 * MIB),
        cost_estimate=pl.CostEstimate(
            flops=2 * rows * q_cols * out_cols,
            bytes_accessed=2 * q_cols * out_cols,
            transcendentals=0,
        ),
        name="output",
    )(in_vmem(w_out), *blocks)

    total = own
    for j in range(1, gy):
        part = lax.ppermute(other[j - 1], "gy", [(i, (i + j) % gy) for i in range(gy)])
        total = total + part.astype(jnp.float32)
    return total.astype(jnp.bfloat16)


def solution(mesh):
    in_specs = (
        P("groups", "gx"),
        P("gx", "gy"),
        P("gx", "gy"),
        P("gx", "gy"),
        P("gy", "gx"),
        P(("groups", "gx"), "gy", None, None),
        P(("groups", "gx"), "gy", None, None),
        P(("groups", "gx")),
    )
    out_specs = P(("groups", "gy"), "gx")
    body = functools.partial(on_device, mesh.shape["gx"], mesh.shape["gy"])
    return jax.shard_map(body, mesh=mesh, in_specs=in_specs, out_specs=out_specs, check_vma=False)
```

```python
import functools

import jax
import jax.numpy as jnp
from jax import lax
from jax.experimental import pallas as pl
from jax.experimental.pallas import tpu as pltpu
from jax.sharding import PartitionSpec as P

rope_base = 500000.0
MIB = 1024 * 1024


def project_kernel(
    near, far, device_at, own, slab, head_dim, tokens_ref, wq_ref, wk_ref, wv_ref, keep_ref, *refs
):
    send_refs = refs[: near - 1]
    t_buf, q_buf, k_buf, v_buf, partial, sems = refs[near - 1 :]
    rows, depth = tokens_ref.shape
    heads = q_buf.shape[1] // head_dim
    kv_heads = wk_ref.shape[1] // head_dim
    t_copy = pltpu.make_async_copy(tokens_ref, t_buf, sems.at[0])
    k_copy = pltpu.make_async_copy(wk_ref, k_buf, sems.at[1])
    v_copy = pltpu.make_async_copy(wv_ref, v_buf, sems.at[2])
    t_copy.start()
    k_copy.start()
    v_copy.start()
    q_copies = []
    for c in range(depth // slab):
        at = slice(c * slab, (c + 1) * slab)
        q_copies.append((pltpu.make_async_copy(wq_ref.at[at, :], q_buf.at[at, :], sems.at[3 + c]), at))
        q_copies[-1][0].start()

    row = lax.broadcasted_iota(jnp.int32, (rows, rows), 0)
    column = lax.broadcasted_iota(jnp.int32, (rows, rows), 1)
    wanted = jnp.zeros((rows, rows), jnp.int32)
    for p in range(near):
        for q in range(far):
            at = p * far + q
            wanted = jnp.where(row >= at * own, row + (device_at(p, q) - at) * own, wanted)
    pick = (column == wanted).astype(jnp.bfloat16)
    t_copy.wait()
    tokens = jnp.dot(pick, t_buf[...], preferred_element_type=jnp.float32).astype(jnp.bfloat16)

    group = far * own

    def put(part, head):
        count = part.shape[1] // head_dim
        for p in range(near):
            ref = send_refs[p - 1] if p else keep_ref
            tiles = [
                part[p * group : (p + 1) * group, h * head_dim : (h + 1) * head_dim] for h in range(count)
            ]
            ref[head * group : (head + count) * group, :] = jnp.concatenate(tiles, axis=0).astype(ref.dtype)

    def times(part, weights):
        return jnp.dot(part, weights, preferred_element_type=jnp.float32)

    k_copy.wait()
    put(times(tokens, k_buf[...]), heads)
    v_copy.wait()
    put(times(tokens, v_buf[...]), heads + kv_heads)
    q_cols = q_buf.shape[1]
    width = q_cols // 4 if q_cols % (4 * head_dim) == 0 else q_cols
    for c, (copy, at) in enumerate(q_copies):
        copy.wait()
        for first in range(0, q_cols, width):
            columns = slice(first, first + width)
            part = times(tokens[:, at], q_buf[at, columns])
            if c > 0:
                part = part + partial[:, columns]
            if c < len(q_copies) - 1:
                partial[:, columns] = part
            else:
                put(part, first // head_dim)


def partner(f, k, far):
    return f ^ k if far & (far - 1) == 0 else (f + k) % far


def source(f, k, far):
    return f ^ k if far & (far - 1) == 0 else (f + far - k) % far


def combine_kernel(steps, heads, kv_heads, cache_ref, keep_ref, *refs):
    received, outs, total_ref = refs[: -steps - 1], refs[-steps - 1 : -1], refs[-1]
    total = keep_ref[...]
    for part in received:
        total = total + part[...].astype(jnp.float32)
    total_ref[...] = total
    own = outs[0].shape[0] // (heads + 2 * kv_heads)
    group = steps * own

    def of_heads(j, first, count):
        return [total_ref[pl.ds(first * group + j * own + r, count, stride=group), :] for r in range(own)]

    for j in range(steps):
        rows = (
            of_heads(j, 0, heads)
            + of_heads(j, heads, kv_heads)
            + of_heads(j, heads + kv_heads, kv_heads)
        )
        outs[j][...] = jnp.concatenate(rows, axis=0).astype(outs[j].dtype)


def attend_kernel(table_ref, keys, values, *refs):
    parts, out_ref = refs[:-1], refs[-1]
    rows, kv_heads, slots, head_dim = keys.shape
    heads = out_ref.shape[0] // rows
    group = heads // kv_heads
    pairs = [(r, k) for r in range(rows) for k in range(kv_heads)]
    total = parts[0][...].astype(jnp.float32)
    for part in parts[1:]:
        total = total + part[...].astype(jnp.float32)
    cosine = table_ref[:rows]
    sine = table_ref[rows : 2 * rows]
    filled = table_ref[2 * rows :]

    def rotated(vectors, count):
        per_row = (rows, count, head_dim)
        c = jnp.broadcast_to(cosine[:, None, :], per_row).reshape(rows * count, head_dim)
        s = jnp.broadcast_to(sine[:, None, :], per_row).reshape(rows * count, head_dim)
        return (vectors * c + pltpu.roll(vectors, head_dim // 2, 1) * s).astype(jnp.bfloat16)

    q_count = rows * heads
    kv_count = rows * kv_heads
    queries = rotated(total[:q_count], heads)
    new_keys = rotated(total[q_count : q_count + kv_count], kv_heads).astype(jnp.float32)
    new_values = total[q_count + kv_count :].astype(jnp.bfloat16).astype(jnp.float32)
    scaling = head_dim ** (-0.5)
    slot = lax.broadcasted_iota(jnp.int32, (group, slots), 1).astype(jnp.float32)
    scores = []
    own_scores = []
    for i, (r, k) in enumerate(pairs):
        q = queries[i * group : (i + 1) * group]
        score = lax.dot_general(
            q, keys[r, k], (((1,), (1,)), ((), ())), preferred_element_type=jnp.float32
        )
        scores.append(jnp.where(slot < filled[r : r + 1, :1], score * scaling, jnp.float32(-1e30)))
        own_scores.append(
            jnp.sum(q.astype(jnp.float32) * new_keys[i : i + 1], axis=1, keepdims=True) * scaling
        )
    highest = [
        jnp.maximum(jnp.max(score, axis=1, keepdims=True), own)
        for score, own in zip(scores, own_scores)
    ]
    weights = [jnp.exp(score - high) for score, high in zip(scores, highest)]
    own_weights = [jnp.exp(own - high) for own, high in zip(own_scores, highest)]
    norms = [
        jnp.sum(weight, axis=1, keepdims=True) + own for weight, own in zip(weights, own_weights)
    ]
    mixed = []
    for i, (r, k) in enumerate(pairs):
        head = jnp.dot(weights[i].astype(jnp.bfloat16), values[r, k], preferred_element_type=jnp.float32)
        mixed.append((head + own_weights[i] * new_values[i : i + 1]) / norms[i])
    out_ref[...] = jnp.concatenate(mixed, axis=0).astype(jnp.bfloat16)


def output_kernel(n, gy, order, w_ref, *refs):
    far = len(order)
    blocks = refs[:far]
    own_ref, other_ref, wide, lhs = refs[far:]
    near, per_dev, head_dim = blocks[0].shape
    heads = w_ref.shape[0] // head_dim
    rows = n * per_dev // heads
    out_cols = w_ref.shape[1]
    width = min(512, out_cols)
    half = n // gy
    me, me_gy = lax.axis_index("gx"), lax.axis_index("gy")
    mine, mine_far = lax.rem(me, near), lax.div(me, near)
    for k in range(far):
        for j in range(near):
            d = source(mine_far, order[k], far) * near + lax.rem(mine + near - j, near)
            place = lax.rem(lax.div(d, half) + gy - me_gy, gy) * half + lax.rem(d, half)
            wide[pl.ds(pl.multiple_of(place * per_dev, per_dev), per_dev), :] = blocks[k][j].astype(jnp.float32)
    for h in range(heads):
        lhs[:, h * head_dim : (h + 1) * head_dim] = wide[pl.ds(h, rows, stride=heads), :].astype(lhs.dtype)
    for c in range(out_cols // width):
        part = jnp.dot(
            lhs[...], w_ref[:, c * width : (c + 1) * width], preferred_element_type=jnp.float32
        )
        own_ref[:, c * width : (c + 1) * width] = part[: rows // gy]
        for j in range(1, gy):
            other = part[j * (rows // gy) : (j + 1) * (rows // gy)]
            other_ref[j - 1, :, c * width : (c + 1) * width] = other.astype(other_ref.dtype)


def in_hbm(x):
    return pltpu.with_memory_space_constraint(x, pltpu.HBM)


def in_vmem(x):
    return pltpu.with_memory_space_constraint(x, pltpu.VMEM)


def on_device(n, gy, tokens, w_query, w_key, w_value, w_out, key_cache, value_cache, lengths):
    own_rows, kv_heads, slots, head_dim = key_cache.shape
    rows, depth = tokens.shape
    q_cols = w_query.shape[1]
    kv_cols = w_key.shape[1]
    heads = q_cols // head_dim
    out_cols = w_out.shape[1]
    vmem = pl.BlockSpec(memory_space=pltpu.VMEM)
    anywhere = pl.BlockSpec(memory_space=pl.ANY)
    block = own_rows * (heads + 2 * kv_heads)

    near = 2 if n % 2 == 0 else 1
    far = n // near
    order_out = sorted(range(1, far), key=lambda k: -(k // 2))
    order_back = sorted(range(1, far), key=lambda k: k % 2)

    def to_near(x, j):
        return lax.ppermute(
            x, "gx", [(f * near + i, f * near + (i + j) % near) for f in range(far) for i in range(near)]
        )

    def to_far(x, k):
        return lax.ppermute(
            x, "gx", [(f * near + i, int(partner(f, k, far)) * near + i) for f in range(far) for i in range(near)]
        )

    slab = 256 if depth % 256 == 0 else depth

    def device_at(j, k):
        me = lax.axis_index("gx")
        return partner(lax.div(me, near), k, far) * near + lax.rem(lax.rem(me, near) + j, near)

    all_heads = heads + 2 * kv_heads
    keep, *sends = pl.pallas_call(
        functools.partial(
            project_kernel, near, far, device_at, own_rows, slab, head_dim
        ),
        out_shape=[
            jax.ShapeDtypeStruct(
                (all_heads * far * own_rows, head_dim), jnp.bfloat16 if p else jnp.float32
            )
            for p in range(near)
        ],
        in_specs=[anywhere, anywhere, anywhere, anywhere],
        out_specs=[vmem] * near,
        scratch_shapes=[
            pltpu.VMEM((rows, depth), jnp.bfloat16),
            pltpu.VMEM((depth, q_cols), jnp.bfloat16),
            pltpu.VMEM((depth, kv_cols), jnp.bfloat16),
            pltpu.VMEM((depth, kv_cols), jnp.bfloat16),
            pltpu.VMEM((rows, q_cols), jnp.float32),
            pltpu.SemaphoreType.DMA((3 + depth // slab,)),
        ],
        compiler_params=pltpu.CompilerParams(vmem_limit_bytes=26 * MIB),
        cost_estimate=pl.CostEstimate(
            flops=2 * rows * depth * (q_cols + 2 * kv_cols),
            bytes_accessed=2 * depth * (q_cols + 2 * kv_cols),
            transcendentals=0,
        ),
        name="project",
    )(in_hbm(tokens), in_hbm(w_query), in_hbm(w_key), in_hbm(w_value))

    received = [to_near(sends[p - 1], p) for p in range(1, near)]

    summed = pl.pallas_call(
        functools.partial(combine_kernel, far, heads, kv_heads),
        out_shape=[
            jax.ShapeDtypeStruct((block, head_dim), jnp.bfloat16 if q else jnp.float32)
            for q in range(far)
        ],
        in_specs=[vmem] * (2 + len(received)),
        out_specs=[vmem] * far,
        scratch_shapes=[pltpu.VMEM((all_heads * far * own_rows, head_dim), jnp.float32)],
        compiler_params=pltpu.CompilerParams(vmem_limit_bytes=12 * MIB),
        cost_estimate=pl.CostEstimate(flops=0, bytes_accessed=16 * MIB, transcendentals=0),
        name="combine",
    )(in_vmem(value_cache), keep, *received)

    parts = [summed[0]] + [to_far(summed[q], q) for q in order_out]

    half = head_dim // 2
    freqs = rope_base ** (-2.0 * jnp.arange(half).astype(jnp.float32) / (2.0 * half))
    positions = lengths.astype(jnp.float32)[:, None]
    angles = positions * freqs[None, :]
    cosine = jnp.cos(angles)
    sine = jnp.sin(angles)
    table = jnp.concatenate(
        [
            jnp.concatenate([cosine, cosine], axis=1),
            jnp.concatenate([-sine, sine], axis=1),
            jnp.broadcast_to(positions, (own_rows, head_dim)),
        ],
        axis=0,
    )

    mixed = pl.pallas_call(
        attend_kernel,
        out_shape=jax.ShapeDtypeStruct((own_rows * heads, head_dim), jnp.bfloat16),
        in_specs=[vmem] * (3 + len(parts)),
        out_specs=vmem,
        compiler_params=pltpu.CompilerParams(vmem_limit_bytes=12 * MIB),
        cost_estimate=pl.CostEstimate(
            flops=4 * own_rows * heads * slots * head_dim,
            bytes_accessed=4 * own_rows * kv_heads * slots * head_dim,
            transcendentals=own_rows * heads * slots,
        ),
        name="attend",
    )(table, in_vmem(key_cache), in_vmem(value_cache), *parts)

    pair = jnp.stack([mixed] + [to_near(mixed, j) for j in range(1, near)])
    blocks = [pair] + [to_far(pair, k) for k in order_back]

    own, other = pl.pallas_call(
        functools.partial(output_kernel, n, gy, (0, *order_back)),
        out_shape=(
            jax.ShapeDtypeStruct((rows // gy, out_cols), jnp.float32),
            jax.ShapeDtypeStruct((gy - 1, rows // gy, out_cols), jnp.bfloat16),
        ),
        in_specs=[vmem] * (1 + far),
        out_specs=(vmem, vmem),
        scratch_shapes=[
            pltpu.VMEM((rows * heads, head_dim), jnp.float32),
            pltpu.VMEM((rows, q_cols), jnp.bfloat16),
        ],
        compiler_params=pltpu.CompilerParams(vmem_limit_bytes=12 * MIB),
        cost_estimate=pl.CostEstimate(
            flops=2 * rows * q_cols * out_cols,
            bytes_accessed=2 * q_cols * out_cols,
            transcendentals=0,
        ),
        name="output",
    )(in_vmem(w_out), *blocks)

    total = own
    for j in range(1, gy):
        part = lax.ppermute(other[j - 1], "gy", [(i, (i + j) % gy) for i in range(gy)])
        total = total + part.astype(jnp.float32)
    return total.astype(jnp.bfloat16)


def solution(mesh):
    in_specs = (
        P("groups", "gx"),
        P("gx", "gy"),
        P("gx", "gy"),
        P("gx", "gy"),
        P("gy", "gx"),
        P(("groups", "gx"), "gy", None, None),
        P(("groups", "gx"), "gy", None, None),
        P(("groups", "gx")),
    )
    out_specs = P(("groups", "gy"), "gx")
    body = functools.partial(on_device, mesh.shape["gx"], mesh.shape["gy"])
    return jax.shard_map(body, mesh=mesh, in_specs=in_specs, out_specs=out_specs, check_vma=False)
```

```python
import functools

import jax
import jax.numpy as jnp
from jax import lax
from jax.experimental import pallas as pl
from jax.experimental.pallas import tpu as pltpu
from jax.sharding import PartitionSpec as P

rope_base = 500000.0
MIB = 1024 * 1024


def project_kernel(
    low, high, device_at, own, slab, head_dim, tokens_ref, wq_ref, wk_ref, wv_ref, keep_ref, *refs
):
    send_refs = refs[: low - 1]
    t_buf, q_buf, k_buf, v_buf, partial, sems = refs[low - 1 :]
    rows, depth = tokens_ref.shape
    heads = q_buf.shape[1] // head_dim
    kv_heads = wk_ref.shape[1] // head_dim
    t_copy = pltpu.make_async_copy(tokens_ref, t_buf, sems.at[0])
    k_copy = pltpu.make_async_copy(wk_ref, k_buf, sems.at[1])
    v_copy = pltpu.make_async_copy(wv_ref, v_buf, sems.at[2])
    t_copy.start()
    k_copy.start()
    v_copy.start()
    q_copies = []
    for c in range(depth // slab):
        at = slice(c * slab, (c + 1) * slab)
        q_copies.append((pltpu.make_async_copy(wq_ref.at[at, :], q_buf.at[at, :], sems.at[3 + c]), at))
        q_copies[-1][0].start()

    row = lax.broadcasted_iota(jnp.int32, (rows, rows), 0)
    column = lax.broadcasted_iota(jnp.int32, (rows, rows), 1)
    wanted = jnp.zeros((rows, rows), jnp.int32)
    for p in range(low):
        for q in range(high):
            at = p * high + q
            wanted = jnp.where(row >= at * own, row + (device_at(p, q) - at) * own, wanted)
    pick = (column == wanted).astype(jnp.bfloat16)
    t_copy.wait()
    tokens = jnp.dot(pick, t_buf[...], preferred_element_type=jnp.float32).astype(jnp.bfloat16)

    group = high * own

    def put(part, head):
        count = part.shape[1] // head_dim
        for p in range(low):
            ref = send_refs[p - 1] if p else keep_ref
            tiles = [
                part[p * group : (p + 1) * group, h * head_dim : (h + 1) * head_dim] for h in range(count)
            ]
            ref[head * group : (head + count) * group, :] = jnp.concatenate(tiles, axis=0).astype(ref.dtype)

    def times(part, weights):
        return jnp.dot(part, weights, preferred_element_type=jnp.float32)

    k_copy.wait()
    put(times(tokens, k_buf[...]), heads)
    v_copy.wait()
    put(times(tokens, v_buf[...]), heads + kv_heads)
    q_cols = q_buf.shape[1]
    width = q_cols // 4 if q_cols % (4 * head_dim) == 0 else q_cols
    for c, (copy, at) in enumerate(q_copies):
        copy.wait()
        for first in range(0, q_cols, width):
            columns = slice(first, first + width)
            part = times(tokens[:, at], q_buf[at, columns])
            if c > 0:
                part = part + partial[:, columns]
            if c < len(q_copies) - 1:
                partial[:, columns] = part
            else:
                put(part, first // head_dim)


def partner(f, k, count):
    return f ^ k if count & (count - 1) == 0 else (f + k) % count


def source(f, k, count):
    return f ^ k if count & (count - 1) == 0 else (f + count - k) % count


def combine_kernel(steps, heads, kv_heads, cache_ref, keep_ref, *refs):
    received, outs, total_ref = refs[: -steps - 1], refs[-steps - 1 : -1], refs[-1]
    total = keep_ref[...]
    for part in received:
        total = total + part[...].astype(jnp.float32)
    total_ref[...] = total
    own = outs[0].shape[0] // (heads + 2 * kv_heads)
    group = steps * own

    def of_heads(j, first, count):
        return [total_ref[pl.ds(first * group + j * own + r, count, stride=group), :] for r in range(own)]

    for j in range(steps):
        rows = (
            of_heads(j, 0, heads)
            + of_heads(j, heads, kv_heads)
            + of_heads(j, heads + kv_heads, kv_heads)
        )
        outs[j][...] = jnp.concatenate(rows, axis=0).astype(outs[j].dtype)


def attend_kernel(table_ref, keys, values, *refs):
    parts, out_ref = refs[:-1], refs[-1]
    rows, kv_heads, slots, head_dim = keys.shape
    heads = out_ref.shape[0] // rows
    group = heads // kv_heads
    pairs = [(r, k) for r in range(rows) for k in range(kv_heads)]
    total = parts[0][...].astype(jnp.float32)
    for part in parts[1:]:
        total = total + part[...].astype(jnp.float32)
    cosine = table_ref[:rows]
    sine = table_ref[rows : 2 * rows]
    filled = table_ref[2 * rows :]

    def rotated(vectors, count):
        per_row = (rows, count, head_dim)
        c = jnp.broadcast_to(cosine[:, None, :], per_row).reshape(rows * count, head_dim)
        s = jnp.broadcast_to(sine[:, None, :], per_row).reshape(rows * count, head_dim)
        return (vectors * c + pltpu.roll(vectors, head_dim // 2, 1) * s).astype(jnp.bfloat16)

    q_count = rows * heads
    kv_count = rows * kv_heads
    queries = rotated(total[:q_count], heads)
    new_keys = rotated(total[q_count : q_count + kv_count], kv_heads).astype(jnp.float32)
    new_values = total[q_count + kv_count :].astype(jnp.bfloat16).astype(jnp.float32)
    scaling = head_dim ** (-0.5)
    slot = lax.broadcasted_iota(jnp.int32, (group, slots), 1).astype(jnp.float32)
    scores = []
    own_scores = []
    for i, (r, k) in enumerate(pairs):
        q = queries[i * group : (i + 1) * group]
        score = lax.dot_general(
            q, keys[r, k], (((1,), (1,)), ((), ())), preferred_element_type=jnp.float32
        )
        scores.append(jnp.where(slot < filled[r : r + 1, :1], score * scaling, jnp.float32(-1e30)))
        own_scores.append(
            jnp.sum(q.astype(jnp.float32) * new_keys[i : i + 1], axis=1, keepdims=True) * scaling
        )
    highest = [
        jnp.maximum(jnp.max(score, axis=1, keepdims=True), own)
        for score, own in zip(scores, own_scores)
    ]
    weights = [jnp.exp(score - high) for score, high in zip(scores, highest)]
    own_weights = [jnp.exp(own - high) for own, high in zip(own_scores, highest)]
    norms = [
        jnp.sum(weight, axis=1, keepdims=True) + own for weight, own in zip(weights, own_weights)
    ]
    mixed = []
    for i, (r, k) in enumerate(pairs):
        head = jnp.dot(weights[i].astype(jnp.bfloat16), values[r, k], preferred_element_type=jnp.float32)
        mixed.append((head + own_weights[i] * new_values[i : i + 1]) / norms[i])
    out_ref[...] = jnp.concatenate(mixed, axis=0).astype(jnp.bfloat16)


def output_kernel(gy, order, w_ref, *refs):
    low = len(order)
    blocks = refs[:low]
    own_ref, other_ref, wide, lhs = refs[low:]
    high, per_dev, head_dim = blocks[0].shape
    heads = w_ref.shape[0] // head_dim
    rows = high * low * per_dev // heads
    out_cols = w_ref.shape[1]
    width = min(512, out_cols)
    half = high * low // gy
    me, me_gy = lax.axis_index("gx"), lax.axis_index("gy")
    for k in range(low):
        for j in range(high):
            d = source(lax.div(me, low), j, high) * low + source(lax.rem(me, low), order[k], low)
            place = lax.rem(lax.div(d, half) + gy - me_gy, gy) * half + lax.rem(d, half)
            wide[pl.ds(pl.multiple_of(place * per_dev, per_dev), per_dev), :] = blocks[k][j].astype(jnp.float32)
    for h in range(heads):
        lhs[:, h * head_dim : (h + 1) * head_dim] = wide[pl.ds(h, rows, stride=heads), :].astype(lhs.dtype)
    for c in range(out_cols // width):
        part = jnp.dot(
            lhs[...], w_ref[:, c * width : (c + 1) * width], preferred_element_type=jnp.float32
        )
        own_ref[:, c * width : (c + 1) * width] = part[: rows // gy]
        for j in range(1, gy):
            other = part[j * (rows // gy) : (j + 1) * (rows // gy)]
            other_ref[j - 1, :, c * width : (c + 1) * width] = other.astype(other_ref.dtype)


def in_hbm(x):
    return pltpu.with_memory_space_constraint(x, pltpu.HBM)


def in_vmem(x):
    return pltpu.with_memory_space_constraint(x, pltpu.VMEM)


def on_device(n, gy, tokens, w_query, w_key, w_value, w_out, key_cache, value_cache, lengths):
    own_rows, kv_heads, slots, head_dim = key_cache.shape
    rows, depth = tokens.shape
    q_cols = w_query.shape[1]
    kv_cols = w_key.shape[1]
    heads = q_cols // head_dim
    out_cols = w_out.shape[1]
    vmem = pl.BlockSpec(memory_space=pltpu.VMEM)
    anywhere = pl.BlockSpec(memory_space=pl.ANY)
    block = own_rows * (heads + 2 * kv_heads)

    low = n
    while low * low >= 4 * n and low % 2 == 0:
        low //= 2
    high = n // low
    order = range(low - 1, 0, -1)

    def to_low(x, k):
        return lax.ppermute(
            x, "gx", [(h * low + i, h * low + int(partner(i, k, low))) for h in range(high) for i in range(low)]
        )

    def to_high(x, k):
        return lax.ppermute(
            x, "gx", [(h * low + i, int(partner(h, k, high)) * low + i) for h in range(high) for i in range(low)]
        )

    slab = 256 if depth % 256 == 0 else depth

    def device_at(p, q):
        me = lax.axis_index("gx")
        return partner(lax.div(me, low), q, high) * low + partner(lax.rem(me, low), p, low)

    all_heads = heads + 2 * kv_heads
    keep, *sends = pl.pallas_call(
        functools.partial(project_kernel, low, high, device_at, own_rows, slab, head_dim),
        out_shape=[
            jax.ShapeDtypeStruct(
                (all_heads * high * own_rows, head_dim), jnp.bfloat16 if p else jnp.float32
            )
            for p in range(low)
        ],
        in_specs=[anywhere, anywhere, anywhere, anywhere],
        out_specs=[vmem] * low,
        scratch_shapes=[
            pltpu.VMEM((rows, depth), jnp.bfloat16),
            pltpu.VMEM((depth, q_cols), jnp.bfloat16),
            pltpu.VMEM((depth, kv_cols), jnp.bfloat16),
            pltpu.VMEM((depth, kv_cols), jnp.bfloat16),
            pltpu.VMEM((rows, q_cols), jnp.float32),
            pltpu.SemaphoreType.DMA((3 + depth // slab,)),
        ],
        compiler_params=pltpu.CompilerParams(vmem_limit_bytes=26 * MIB),
        cost_estimate=pl.CostEstimate(
            flops=2 * rows * depth * (q_cols + 2 * kv_cols),
            bytes_accessed=2 * depth * (q_cols + 2 * kv_cols),
            transcendentals=0,
        ),
        name="project",
    )(in_hbm(tokens), in_hbm(w_query), in_hbm(w_key), in_hbm(w_value))

    received = [to_low(sends[p - 1], p) for p in order]

    summed = pl.pallas_call(
        functools.partial(combine_kernel, high, heads, kv_heads),
        out_shape=[
            jax.ShapeDtypeStruct((block, head_dim), jnp.bfloat16 if q else jnp.float32)
            for q in range(high)
        ],
        in_specs=[vmem] * (2 + len(received)),
        out_specs=[vmem] * high,
        scratch_shapes=[pltpu.VMEM((all_heads * high * own_rows, head_dim), jnp.float32)],
        compiler_params=pltpu.CompilerParams(vmem_limit_bytes=12 * MIB),
        cost_estimate=pl.CostEstimate(flops=0, bytes_accessed=16 * MIB, transcendentals=0),
        name="combine",
    )(in_vmem(value_cache), keep, *received)

    parts = [summed[0]] + [to_high(summed[q], q) for q in range(1, high)]

    half = head_dim // 2
    freqs = rope_base ** (-2.0 * jnp.arange(half).astype(jnp.float32) / (2.0 * half))
    positions = lengths.astype(jnp.float32)[:, None]
    angles = positions * freqs[None, :]
    cosine = jnp.cos(angles)
    sine = jnp.sin(angles)
    table = jnp.concatenate(
        [
            jnp.concatenate([cosine, cosine], axis=1),
            jnp.concatenate([-sine, sine], axis=1),
            jnp.broadcast_to(positions, (own_rows, head_dim)),
        ],
        axis=0,
    )

    mixed = pl.pallas_call(
        attend_kernel,
        out_shape=jax.ShapeDtypeStruct((own_rows * heads, head_dim), jnp.bfloat16),
        in_specs=[vmem] * (3 + len(parts)),
        out_specs=vmem,
        compiler_params=pltpu.CompilerParams(vmem_limit_bytes=12 * MIB),
        cost_estimate=pl.CostEstimate(
            flops=4 * own_rows * heads * slots * head_dim,
            bytes_accessed=4 * own_rows * kv_heads * slots * head_dim,
            transcendentals=own_rows * heads * slots,
        ),
        name="attend",
    )(table, in_vmem(key_cache), in_vmem(value_cache), *parts)

    column = jnp.stack([mixed] + [to_high(mixed, q) for q in range(1, high)])
    blocks = [column] + [to_low(column, k) for k in order]

    own, other = pl.pallas_call(
        functools.partial(output_kernel, gy, (0, *order)),
        out_shape=(
            jax.ShapeDtypeStruct((rows // gy, out_cols), jnp.float32),
            jax.ShapeDtypeStruct((gy - 1, rows // gy, out_cols), jnp.bfloat16),
        ),
        in_specs=[vmem] * (1 + low),
        out_specs=(vmem, vmem),
        scratch_shapes=[
            pltpu.VMEM((rows * heads, head_dim), jnp.float32),
            pltpu.VMEM((rows, q_cols), jnp.bfloat16),
        ],
        compiler_params=pltpu.CompilerParams(vmem_limit_bytes=12 * MIB),
        cost_estimate=pl.CostEstimate(
            flops=2 * rows * q_cols * out_cols,
            bytes_accessed=2 * q_cols * out_cols,
            transcendentals=0,
        ),
        name="output",
    )(in_vmem(w_out), *blocks)

    total = own
    for j in range(1, gy):
        part = lax.ppermute(other[j - 1], "gy", [(i, (i + j) % gy) for i in range(gy)])
        total = total + part.astype(jnp.float32)
    return total.astype(jnp.bfloat16)


def solution(mesh):
    in_specs = (
        P("groups", "gx"),
        P("gx", "gy"),
        P("gx", "gy"),
        P("gx", "gy"),
        P("gy", "gx"),
        P(("groups", "gx"), "gy", None, None),
        P(("groups", "gx"), "gy", None, None),
        P(("groups", "gx")),
    )
    out_specs = P(("groups", "gy"), "gx")
    body = functools.partial(on_device, mesh.shape["gx"], mesh.shape["gy"])
    return jax.shard_map(body, mesh=mesh, in_specs=in_specs, out_specs=out_specs, check_vma=False)
```

```python
import functools

import jax
import jax.numpy as jnp
from jax import lax
from jax.experimental import pallas as pl
from jax.experimental.pallas import tpu as pltpu
from jax.sharding import PartitionSpec as P

rope_base = 500000.0
MIB = 1024 * 1024


def project_kernel(
    low, high, device_at, own, slab, head_dim, tokens_ref, wq_ref, wk_ref, wv_ref, keep_ref, *refs
):
    send_refs = refs[: low - 1]
    t_buf, q_buf, k_buf, v_buf, partial, sems = refs[low - 1 :]
    rows, depth = tokens_ref.shape
    heads = q_buf.shape[1] // head_dim
    kv_heads = wk_ref.shape[1] // head_dim
    t_copy = pltpu.make_async_copy(tokens_ref, t_buf, sems.at[0])
    k_copy = pltpu.make_async_copy(wk_ref, k_buf, sems.at[1])
    v_copy = pltpu.make_async_copy(wv_ref, v_buf, sems.at[2])
    t_copy.start()
    k_copy.start()
    v_copy.start()
    q_copies = []
    for c in range(depth // slab):
        at = slice(c * slab, (c + 1) * slab)
        q_copies.append((pltpu.make_async_copy(wq_ref.at[at, :], q_buf.at[at, :], sems.at[3 + c]), at))
        q_copies[-1][0].start()

    row = lax.broadcasted_iota(jnp.int32, (rows, rows), 0)
    column = lax.broadcasted_iota(jnp.int32, (rows, rows), 1)
    wanted = jnp.zeros((rows, rows), jnp.int32)
    for p in range(low):
        for q in range(high):
            at = p * high + q
            wanted = jnp.where(row >= at * own, row + (device_at(p, q) - at) * own, wanted)
    pick = (column == wanted).astype(jnp.bfloat16)
    t_copy.wait()
    tokens = jnp.dot(pick, t_buf[...], preferred_element_type=jnp.float32).astype(jnp.bfloat16)

    group = high * own

    def put(part, head):
        count = part.shape[1] // head_dim
        for p in range(low):
            ref = send_refs[p - 1] if p else keep_ref
            tiles = [
                part[p * group : (p + 1) * group, h * head_dim : (h + 1) * head_dim] for h in range(count)
            ]
            ref[head * group : (head + count) * group, :] = jnp.concatenate(tiles, axis=0).astype(ref.dtype)

    def times(part, weights):
        return jnp.dot(part, weights, preferred_element_type=jnp.float32)

    k_copy.wait()
    put(times(tokens, k_buf[...]), heads)
    v_copy.wait()
    put(times(tokens, v_buf[...]), heads + kv_heads)
    q_cols = q_buf.shape[1]
    width = q_cols // 4 if q_cols % (4 * head_dim) == 0 else q_cols
    for c, (copy, at) in enumerate(q_copies):
        copy.wait()
        for first in range(0, q_cols, width):
            columns = slice(first, first + width)
            part = times(tokens[:, at], q_buf[at, columns])
            if c > 0:
                part = part + partial[:, columns]
            if c < len(q_copies) - 1:
                partial[:, columns] = part
            else:
                put(part, first // head_dim)


def partner(f, k, count):
    return f ^ k if count & (count - 1) == 0 else (f + k) % count


def source(f, k, count):
    return f ^ k if count & (count - 1) == 0 else (f + count - k) % count


def combine_kernel(steps, heads, kv_heads, cache_ref, keep_ref, *refs):
    received, outs, total_ref = refs[: -steps - 1], refs[-steps - 1 : -1], refs[-1]
    total = keep_ref[...]
    for part in received:
        total = total + part[...].astype(jnp.float32)
    total_ref[...] = total
    own = outs[0].shape[0] // (heads + 2 * kv_heads)
    group = steps * own

    def of_heads(j, first, count):
        return [total_ref[pl.ds(first * group + j * own + r, count, stride=group), :] for r in range(own)]

    for j in range(steps):
        rows = (
            of_heads(j, 0, heads)
            + of_heads(j, heads, kv_heads)
            + of_heads(j, heads + kv_heads, kv_heads)
        )
        outs[j][...] = jnp.concatenate(rows, axis=0).astype(outs[j].dtype)


def attend_kernel(table_ref, keys, values, *refs):
    parts, out_ref = refs[:-1], refs[-1]
    rows, kv_heads, slots, head_dim = keys.shape
    heads = out_ref.shape[0] // rows
    group = heads // kv_heads
    pairs = [(r, k) for r in range(rows) for k in range(kv_heads)]
    total = parts[0][...].astype(jnp.float32)
    for part in parts[1:]:
        total = total + part[...].astype(jnp.float32)
    cosine = table_ref[:rows]
    sine = table_ref[rows : 2 * rows]
    filled = table_ref[2 * rows :]

    def rotated(vectors, count):
        per_row = (rows, count, head_dim)
        c = jnp.broadcast_to(cosine[:, None, :], per_row).reshape(rows * count, head_dim)
        s = jnp.broadcast_to(sine[:, None, :], per_row).reshape(rows * count, head_dim)
        return (vectors * c + pltpu.roll(vectors, head_dim // 2, 1) * s).astype(jnp.bfloat16)

    q_count = rows * heads
    kv_count = rows * kv_heads
    queries = rotated(total[:q_count], heads)
    new_keys = rotated(total[q_count : q_count + kv_count], kv_heads).astype(jnp.float32)
    new_values = total[q_count + kv_count :].astype(jnp.bfloat16).astype(jnp.float32)
    scaling = head_dim ** (-0.5)
    slot = lax.broadcasted_iota(jnp.int32, (group, slots), 1).astype(jnp.float32)
    scores = []
    own_scores = []
    for i, (r, k) in enumerate(pairs):
        q = queries[i * group : (i + 1) * group]
        score = lax.dot_general(
            q, keys[r, k], (((1,), (1,)), ((), ())), preferred_element_type=jnp.float32
        )
        scores.append(jnp.where(slot < filled[r : r + 1, :1], score * scaling, jnp.float32(-1e30)))
        own_scores.append(
            jnp.sum(q.astype(jnp.float32) * new_keys[i : i + 1], axis=1, keepdims=True) * scaling
        )
    highest = [
        jnp.maximum(jnp.max(score, axis=1, keepdims=True), own)
        for score, own in zip(scores, own_scores)
    ]
    weights = [jnp.exp(score - high) for score, high in zip(scores, highest)]
    own_weights = [jnp.exp(own - high) for own, high in zip(own_scores, highest)]
    norms = [
        jnp.sum(weight, axis=1, keepdims=True) + own for weight, own in zip(weights, own_weights)
    ]
    mixed = []
    for i, (r, k) in enumerate(pairs):
        head = jnp.dot(weights[i].astype(jnp.bfloat16), values[r, k], preferred_element_type=jnp.float32)
        mixed.append((head + own_weights[i] * new_values[i : i + 1]) / norms[i])
    out_ref[...] = jnp.concatenate(mixed, axis=0).astype(jnp.bfloat16)


def fill_rows(x):
    rows = x.shape[0]
    return jnp.concatenate([x] * (128 // rows), axis=0) if rows < 128 and 128 % rows == 0 else x


def output_kernel(gy, order, w_ref, *refs):
    low = len(order)
    blocks = refs[:low]
    own_ref, other_ref, wide, lhs = refs[low:]
    high, per_dev, head_dim = blocks[0].shape
    heads = w_ref.shape[0] // head_dim
    rows = high * low * per_dev // heads
    out_cols = w_ref.shape[1]
    width = min(512, out_cols)
    half = high * low // gy
    me, me_gy = lax.axis_index("gx"), lax.axis_index("gy")
    for k in range(low):
        for j in range(high):
            d = source(lax.div(me, low), j, high) * low + source(lax.rem(me, low), order[k], low)
            place = lax.rem(lax.div(d, half) + gy - me_gy, gy) * half + lax.rem(d, half)
            wide[pl.ds(pl.multiple_of(place * per_dev, per_dev), per_dev), :] = blocks[k][j].astype(jnp.float32)
    for h in range(heads):
        lhs[:, h * head_dim : (h + 1) * head_dim] = wide[pl.ds(h, rows, stride=heads), :].astype(lhs.dtype)
    filled = fill_rows(lhs[...])
    for c in range(out_cols // width):
        part = jnp.dot(
            filled, w_ref[:, c * width : (c + 1) * width], preferred_element_type=jnp.float32
        )
        own_ref[:, c * width : (c + 1) * width] = part[: rows // gy]
        for j in range(1, gy):
            other = part[j * (rows // gy) : (j + 1) * (rows // gy)]
            other_ref[j - 1, :, c * width : (c + 1) * width] = other.astype(other_ref.dtype)


def in_hbm(x):
    return pltpu.with_memory_space_constraint(x, pltpu.HBM)


def in_vmem(x):
    return pltpu.with_memory_space_constraint(x, pltpu.VMEM)


def on_device(n, gy, tokens, w_query, w_key, w_value, w_out, key_cache, value_cache, lengths):
    own_rows, kv_heads, slots, head_dim = key_cache.shape
    rows, depth = tokens.shape
    q_cols = w_query.shape[1]
    kv_cols = w_key.shape[1]
    heads = q_cols // head_dim
    out_cols = w_out.shape[1]
    vmem = pl.BlockSpec(memory_space=pltpu.VMEM)
    anywhere = pl.BlockSpec(memory_space=pl.ANY)
    block = own_rows * (heads + 2 * kv_heads)

    low = n
    while low * low >= 4 * n and low % 2 == 0:
        low //= 2
    high = n // low
    order = range(low - 1, 0, -1)

    def to_low(x, k):
        return lax.ppermute(
            x, "gx", [(h * low + i, h * low + int(partner(i, k, low))) for h in range(high) for i in range(low)]
        )

    def to_high(x, k):
        return lax.ppermute(
            x, "gx", [(h * low + i, int(partner(h, k, high)) * low + i) for h in range(high) for i in range(low)]
        )

    slab = 256 if depth % 256 == 0 else depth

    def device_at(p, q):
        me = lax.axis_index("gx")
        return partner(lax.div(me, low), q, high) * low + partner(lax.rem(me, low), p, low)

    all_heads = heads + 2 * kv_heads
    keep, *sends = pl.pallas_call(
        functools.partial(project_kernel, low, high, device_at, own_rows, slab, head_dim),
        out_shape=[
            jax.ShapeDtypeStruct(
                (all_heads * high * own_rows, head_dim), jnp.bfloat16 if p else jnp.float32
            )
            for p in range(low)
        ],
        in_specs=[anywhere, anywhere, anywhere, anywhere],
        out_specs=[vmem] * low,
        scratch_shapes=[
            pltpu.VMEM((rows, depth), jnp.bfloat16),
            pltpu.VMEM((depth, q_cols), jnp.bfloat16),
            pltpu.VMEM((depth, kv_cols), jnp.bfloat16),
            pltpu.VMEM((depth, kv_cols), jnp.bfloat16),
            pltpu.VMEM((rows, q_cols), jnp.float32),
            pltpu.SemaphoreType.DMA((3 + depth // slab,)),
        ],
        compiler_params=pltpu.CompilerParams(vmem_limit_bytes=26 * MIB),
        cost_estimate=pl.CostEstimate(
            flops=2 * rows * depth * (q_cols + 2 * kv_cols),
            bytes_accessed=2 * depth * (q_cols + 2 * kv_cols),
            transcendentals=0,
        ),
        name="project",
    )(in_hbm(tokens), in_hbm(w_query), in_hbm(w_key), in_hbm(w_value))

    received = [to_low(sends[p - 1], p) for p in order]

    summed = pl.pallas_call(
        functools.partial(combine_kernel, high, heads, kv_heads),
        out_shape=[
            jax.ShapeDtypeStruct((block, head_dim), jnp.bfloat16 if q else jnp.float32)
            for q in range(high)
        ],
        in_specs=[vmem] * (2 + len(received)),
        out_specs=[vmem] * high,
        scratch_shapes=[pltpu.VMEM((all_heads * high * own_rows, head_dim), jnp.float32)],
        compiler_params=pltpu.CompilerParams(vmem_limit_bytes=12 * MIB),
        cost_estimate=pl.CostEstimate(flops=0, bytes_accessed=16 * MIB, transcendentals=0),
        name="combine",
    )(in_vmem(value_cache), keep, *received)

    parts = [summed[0]] + [to_high(summed[q], q) for q in range(1, high)]

    half = head_dim // 2
    freqs = rope_base ** (-2.0 * jnp.arange(half).astype(jnp.float32) / (2.0 * half))
    positions = lengths.astype(jnp.float32)[:, None]
    angles = positions * freqs[None, :]
    cosine = jnp.cos(angles)
    sine = jnp.sin(angles)
    table = jnp.concatenate(
        [
            jnp.concatenate([cosine, cosine], axis=1),
            jnp.concatenate([-sine, sine], axis=1),
            jnp.broadcast_to(positions, (own_rows, head_dim)),
        ],
        axis=0,
    )

    mixed = pl.pallas_call(
        attend_kernel,
        out_shape=jax.ShapeDtypeStruct((own_rows * heads, head_dim), jnp.bfloat16),
        in_specs=[vmem] * (3 + len(parts)),
        out_specs=vmem,
        compiler_params=pltpu.CompilerParams(vmem_limit_bytes=12 * MIB),
        cost_estimate=pl.CostEstimate(
            flops=4 * own_rows * heads * slots * head_dim,
            bytes_accessed=4 * own_rows * kv_heads * slots * head_dim,
            transcendentals=own_rows * heads * slots,
        ),
        name="attend",
    )(table, in_vmem(key_cache), in_vmem(value_cache), *parts)

    column = jnp.stack([mixed] + [to_high(mixed, q) for q in range(1, high)])
    blocks = [column] + [to_low(column, k) for k in order]

    own, other = pl.pallas_call(
        functools.partial(output_kernel, gy, (0, *order)),
        out_shape=(
            jax.ShapeDtypeStruct((rows // gy, out_cols), jnp.float32),
            jax.ShapeDtypeStruct((gy - 1, rows // gy, out_cols), jnp.bfloat16),
        ),
        in_specs=[vmem] * (1 + low),
        out_specs=(vmem, vmem),
        scratch_shapes=[
            pltpu.VMEM((rows * heads, head_dim), jnp.float32),
            pltpu.VMEM((rows, q_cols), jnp.bfloat16),
        ],
        compiler_params=pltpu.CompilerParams(vmem_limit_bytes=12 * MIB),
        cost_estimate=pl.CostEstimate(
            flops=2 * rows * q_cols * out_cols,
            bytes_accessed=2 * q_cols * out_cols,
            transcendentals=0,
        ),
        name="output",
    )(in_vmem(w_out), *blocks)

    total = own
    for j in range(1, gy):
        part = lax.ppermute(other[j - 1], "gy", [(i, (i + j) % gy) for i in range(gy)])
        total = total + part.astype(jnp.float32)
    return total.astype(jnp.bfloat16)


def solution(mesh):
    in_specs = (
        P("groups", "gx"),
        P("gx", "gy"),
        P("gx", "gy"),
        P("gx", "gy"),
        P("gy", "gx"),
        P(("groups", "gx"), "gy", None, None),
        P(("groups", "gx"), "gy", None, None),
        P(("groups", "gx")),
    )
    out_specs = P(("groups", "gy"), "gx")
    body = functools.partial(on_device, mesh.shape["gx"], mesh.shape["gy"])
    return jax.shard_map(body, mesh=mesh, in_specs=in_specs, out_specs=out_specs, check_vma=False)
```

```python
import functools

import jax
import jax.numpy as jnp
from jax import lax
from jax.experimental import pallas as pl
from jax.experimental.pallas import tpu as pltpu
from jax.sharding import PartitionSpec as P

rope_base = 500000.0
MIB = 1024 * 1024


def project_kernel(
    low, high, device_at, own, slab, head_dim, tokens_ref, wq_ref, wk_ref, wv_ref, keep_ref, *refs
):
    send_refs = refs[: low - 1]
    t_buf, q_buf, k_buf, v_buf, partial, sems = refs[low - 1 :]
    rows, depth = tokens_ref.shape
    heads = q_buf.shape[1] // head_dim
    kv_heads = wk_ref.shape[1] // head_dim
    t_copy = pltpu.make_async_copy(tokens_ref, t_buf, sems.at[0])
    k_copy = pltpu.make_async_copy(wk_ref, k_buf, sems.at[1])
    v_copy = pltpu.make_async_copy(wv_ref, v_buf, sems.at[2])
    t_copy.start()
    k_copy.start()
    v_copy.start()
    q_copies = []
    for c in range(depth // slab):
        at = slice(c * slab, (c + 1) * slab)
        q_copies.append((pltpu.make_async_copy(wq_ref.at[at, :], q_buf.at[at, :], sems.at[3 + c]), at))
        q_copies[-1][0].start()

    row = lax.broadcasted_iota(jnp.int32, (rows, rows), 0)
    column = lax.broadcasted_iota(jnp.int32, (rows, rows), 1)
    wanted = jnp.zeros((rows, rows), jnp.int32)
    for p in range(low):
        for q in range(high):
            at = p * high + q
            wanted = jnp.where(row >= at * own, row + (device_at(p, q) - at) * own, wanted)
    pick = (column == wanted).astype(jnp.bfloat16)
    t_copy.wait()
    tokens = jnp.dot(pick, t_buf[...], preferred_element_type=jnp.float32).astype(jnp.bfloat16)

    group = high * own

    def put(part, head):
        count = part.shape[1] // head_dim
        for p in range(low):
            ref = send_refs[p - 1] if p else keep_ref
            tiles = [
                part[p * group : (p + 1) * group, h * head_dim : (h + 1) * head_dim] for h in range(count)
            ]
            ref[head * group : (head + count) * group, :] = jnp.concatenate(tiles, axis=0).astype(ref.dtype)

    def times(part, weights):
        return jnp.dot(part, weights, preferred_element_type=jnp.float32)

    k_copy.wait()
    put(times(tokens, k_buf[...]), heads)
    v_copy.wait()
    put(times(tokens, v_buf[...]), heads + kv_heads)
    q_cols = q_buf.shape[1]
    width = q_cols // 4 if q_cols % (4 * head_dim) == 0 else q_cols
    for c, (copy, at) in enumerate(q_copies):
        copy.wait()
        for first in range(0, q_cols, width):
            columns = slice(first, first + width)
            part = times(tokens[:, at], q_buf[at, columns])
            if c > 0:
                part = part + partial[:, columns]
            if c < len(q_copies) - 1:
                partial[:, columns] = part
            else:
                put(part, first // head_dim)


def partner(f, k, count):
    return f ^ k if count & (count - 1) == 0 else (f + k) % count


def source(f, k, count):
    return f ^ k if count & (count - 1) == 0 else (f + count - k) % count


def combine_kernel(steps, heads, kv_heads, cache_ref, keep_ref, *refs):
    received, outs, total_ref = refs[: -steps - 1], refs[-steps - 1 : -1], refs[-1]
    total = keep_ref[...]
    for part in received:
        total = total + part[...].astype(jnp.float32)
    total_ref[: total.shape[0], :] = total
    own = outs[0].shape[0] // (heads + 2 * kv_heads)
    group = steps * own

    def of_heads(j, first, count):
        return [total_ref[pl.ds(first * group + j * own + r, count, stride=group), :] for r in range(own)]

    for j in range(steps):
        rows = (
            of_heads(j, 0, heads)
            + of_heads(j, heads, kv_heads)
            + of_heads(j, heads + kv_heads, kv_heads)
        )
        outs[j][...] = jnp.concatenate(rows, axis=0).astype(outs[j].dtype)


def attend_kernel(table_ref, keys, values, *refs):
    parts, out_ref = refs[:-1], refs[-1]
    rows, kv_heads, slots, head_dim = keys.shape
    heads = out_ref.shape[0] // rows
    group = heads // kv_heads
    pairs = [(r, k) for r in range(rows) for k in range(kv_heads)]
    total = parts[0][...].astype(jnp.float32)
    for part in parts[1:]:
        total = total + part[...].astype(jnp.float32)
    tile = table_ref.shape[0] // 3
    cosine = table_ref[:tile][:rows]
    sine = table_ref[tile : 2 * tile][:rows]
    filled = table_ref[2 * tile :][:rows]

    def rotated(vectors, count):
        per_row = (rows, count, head_dim)
        c = jnp.broadcast_to(cosine[:, None, :], per_row).reshape(rows * count, head_dim)
        s = jnp.broadcast_to(sine[:, None, :], per_row).reshape(rows * count, head_dim)
        return (vectors * c + pltpu.roll(vectors, head_dim // 2, 1) * s).astype(jnp.bfloat16)

    q_count = rows * heads
    kv_count = rows * kv_heads
    queries = rotated(total[:q_count], heads)
    new_keys = rotated(total[q_count : q_count + kv_count], kv_heads).astype(jnp.float32)
    new_values = total[q_count + kv_count :].astype(jnp.bfloat16).astype(jnp.float32)
    scaling = head_dim ** (-0.5)
    slot = lax.broadcasted_iota(jnp.int32, (group, slots), 1).astype(jnp.float32)
    scores = []
    own_scores = []
    for i, (r, k) in enumerate(pairs):
        q = queries[i * group : (i + 1) * group]
        score = lax.dot_general(
            q, keys[r, k], (((1,), (1,)), ((), ())), preferred_element_type=jnp.float32
        )
        scores.append(jnp.where(slot < filled[r : r + 1, :1], score * scaling, jnp.float32(-1e30)))
        own_scores.append(
            jnp.sum(q.astype(jnp.float32) * new_keys[i : i + 1], axis=1, keepdims=True) * scaling
        )
    highest = [
        jnp.maximum(jnp.max(score, axis=1, keepdims=True), own)
        for score, own in zip(scores, own_scores)
    ]
    weights = [jnp.exp(score - high) for score, high in zip(scores, highest)]
    own_weights = [jnp.exp(own - high) for own, high in zip(own_scores, highest)]
    norms = [
        jnp.sum(weight, axis=1, keepdims=True) + own for weight, own in zip(weights, own_weights)
    ]
    mixed = []
    for i, (r, k) in enumerate(pairs):
        head = jnp.dot(weights[i].astype(jnp.bfloat16), values[r, k], preferred_element_type=jnp.float32)
        mixed.append((head + own_weights[i] * new_values[i : i + 1]) / norms[i])
    out_ref[...] = jnp.concatenate(mixed, axis=0).astype(jnp.bfloat16)


def fill_rows(x):
    rows = x.shape[0]
    return jnp.concatenate([x] * (128 // rows), axis=0) if rows < 128 and 128 % rows == 0 else x


def output_kernel(gy, order, w_ref, *refs):
    low = len(order)
    blocks = refs[:low]
    own_ref, other_ref, wide, lhs = refs[low:]
    high, per_dev, head_dim = blocks[0].shape
    heads = w_ref.shape[0] // head_dim
    rows = high * low * per_dev // heads
    out_cols = w_ref.shape[1]
    width = min(512, out_cols)
    half = high * low // gy
    me, me_gy = lax.axis_index("gx"), lax.axis_index("gy")
    for k in range(low):
        for j in range(high):
            d = source(lax.div(me, low), j, high) * low + source(lax.rem(me, low), order[k], low)
            place = lax.rem(lax.div(d, half) + gy - me_gy, gy) * half + lax.rem(d, half)
            wide[pl.ds(pl.multiple_of(place * per_dev, per_dev), per_dev), :] = blocks[k][j].astype(jnp.float32)
    for h in range(heads):
        lhs[:, h * head_dim : (h + 1) * head_dim] = wide[pl.ds(h, rows, stride=heads), :].astype(lhs.dtype)
    filled = fill_rows(lhs[...])
    for c in range(out_cols // width):
        part = jnp.dot(
            filled, w_ref[:, c * width : (c + 1) * width], preferred_element_type=jnp.float32
        )
        own_ref[:, c * width : (c + 1) * width] = part[: rows // gy]
        for j in range(1, gy):
            other = part[j * (rows // gy) : (j + 1) * (rows // gy)]
            other_ref[j - 1, :, c * width : (c + 1) * width] = other.astype(other_ref.dtype)


def in_hbm(x):
    return pltpu.with_memory_space_constraint(x, pltpu.HBM)


def in_vmem(x):
    return pltpu.with_memory_space_constraint(x, pltpu.VMEM)


def on_device(n, gy, tokens, w_query, w_key, w_value, w_out, key_cache, value_cache, lengths):
    own_rows, kv_heads, slots, head_dim = key_cache.shape
    rows, depth = tokens.shape
    q_cols = w_query.shape[1]
    kv_cols = w_key.shape[1]
    heads = q_cols // head_dim
    out_cols = w_out.shape[1]
    vmem = pl.BlockSpec(memory_space=pltpu.VMEM)
    anywhere = pl.BlockSpec(memory_space=pl.ANY)
    block = own_rows * (heads + 2 * kv_heads)

    low = n
    while low * low >= 4 * n and low % 2 == 0:
        low //= 2
    high = n // low
    order = range(low - 1, 0, -1)

    def to_low(x, k):
        return lax.ppermute(
            x, "gx", [(h * low + i, h * low + int(partner(i, k, low))) for h in range(high) for i in range(low)]
        )

    def to_high(x, k):
        return lax.ppermute(
            x, "gx", [(h * low + i, int(partner(h, k, high)) * low + i) for h in range(high) for i in range(low)]
        )

    slab = 256 if depth % 256 == 0 else depth

    def device_at(p, q):
        me = lax.axis_index("gx")
        return partner(lax.div(me, low), q, high) * low + partner(lax.rem(me, low), p, low)

    all_heads = heads + 2 * kv_heads
    keep, *sends = pl.pallas_call(
        functools.partial(project_kernel, low, high, device_at, own_rows, slab, head_dim),
        out_shape=[
            jax.ShapeDtypeStruct(
                (all_heads * high * own_rows, head_dim), jnp.bfloat16 if p else jnp.float32
            )
            for p in range(low)
        ],
        in_specs=[anywhere, anywhere, anywhere, anywhere],
        out_specs=[vmem] * low,
        scratch_shapes=[
            pltpu.VMEM((rows, depth), jnp.bfloat16),
            pltpu.VMEM((depth, q_cols), jnp.bfloat16),
            pltpu.VMEM((depth, kv_cols), jnp.bfloat16),
            pltpu.VMEM((depth, kv_cols), jnp.bfloat16),
            pltpu.VMEM((rows, q_cols), jnp.float32),
            pltpu.SemaphoreType.DMA((3 + depth // slab,)),
        ],
        compiler_params=pltpu.CompilerParams(vmem_limit_bytes=26 * MIB),
        cost_estimate=pl.CostEstimate(
            flops=2 * rows * depth * (q_cols + 2 * kv_cols),
            bytes_accessed=2 * depth * (q_cols + 2 * kv_cols),
            transcendentals=0,
        ),
        name="project",
    )(in_hbm(tokens), in_hbm(w_query), in_hbm(w_key), in_hbm(w_value))

    received = [to_low(sends[p - 1], p) for p in order]

    summed = pl.pallas_call(
        functools.partial(combine_kernel, high, heads, kv_heads),
        out_shape=[
            jax.ShapeDtypeStruct((block, head_dim), jnp.bfloat16 if q else jnp.float32)
            for q in range(high)
        ],
        in_specs=[vmem] * (2 + len(received)),
        out_specs=[vmem] * high,
        scratch_shapes=[pltpu.VMEM(((all_heads + 8) * high * own_rows, head_dim), jnp.float32)],
        compiler_params=pltpu.CompilerParams(vmem_limit_bytes=12 * MIB),
        cost_estimate=pl.CostEstimate(flops=0, bytes_accessed=16 * MIB, transcendentals=0),
        name="combine",
    )(in_vmem(value_cache), keep, *received)

    parts = [summed[0]] + [to_high(summed[q], q) for q in range(1, high)]

    half = head_dim // 2
    freqs = rope_base ** (-2.0 * jnp.arange(half).astype(jnp.float32) / (2.0 * half))
    positions = jnp.pad(lengths.astype(jnp.float32), (0, -own_rows % 8))[:, None]
    angles = positions * freqs[None, :]
    cosine = jnp.cos(angles)
    sine = jnp.sin(angles)
    table = jnp.concatenate(
        [
            jnp.concatenate([cosine, cosine], axis=1),
            jnp.concatenate([-sine, sine], axis=1),
            jnp.broadcast_to(positions, (positions.shape[0], head_dim)),
        ],
        axis=0,
    )

    mixed = pl.pallas_call(
        attend_kernel,
        out_shape=jax.ShapeDtypeStruct((own_rows * heads, head_dim), jnp.bfloat16),
        in_specs=[vmem] * (3 + len(parts)),
        out_specs=vmem,
        compiler_params=pltpu.CompilerParams(vmem_limit_bytes=12 * MIB),
        cost_estimate=pl.CostEstimate(
            flops=4 * own_rows * heads * slots * head_dim,
            bytes_accessed=4 * own_rows * kv_heads * slots * head_dim,
            transcendentals=own_rows * heads * slots,
        ),
        name="attend",
    )(table, in_vmem(key_cache), in_vmem(value_cache), *parts)

    column = jnp.stack([mixed] + [to_high(mixed, q) for q in range(1, high)])
    blocks = [column] + [to_low(column, k) for k in order]

    own, other = pl.pallas_call(
        functools.partial(output_kernel, gy, (0, *order)),
        out_shape=(
            jax.ShapeDtypeStruct((rows // gy, out_cols), jnp.float32),
            jax.ShapeDtypeStruct((gy - 1, rows // gy, out_cols), jnp.bfloat16),
        ),
        in_specs=[vmem] * (1 + low),
        out_specs=(vmem, vmem),
        scratch_shapes=[
            pltpu.VMEM(((rows + 1) * heads, head_dim), jnp.float32),
            pltpu.VMEM((rows, q_cols), jnp.bfloat16),
        ],
        compiler_params=pltpu.CompilerParams(vmem_limit_bytes=12 * MIB),
        cost_estimate=pl.CostEstimate(
            flops=2 * rows * q_cols * out_cols,
            bytes_accessed=2 * q_cols * out_cols,
            transcendentals=0,
        ),
        name="output",
    )(in_vmem(w_out), *blocks)

    total = own
    for j in range(1, gy):
        part = lax.ppermute(other[j - 1], "gy", [(i, (i + j) % gy) for i in range(gy)])
        total = total + part.astype(jnp.float32)
    return total.astype(jnp.bfloat16)


def solution(mesh):
    in_specs = (
        P("groups", "gx"),
        P("gx", "gy"),
        P("gx", "gy"),
        P("gx", "gy"),
        P("gy", "gx"),
        P(("groups", "gx"), "gy", None, None),
        P(("groups", "gx"), "gy", None, None),
        P(("groups", "gx")),
    )
    out_specs = P(("groups", "gy"), "gx")
    body = functools.partial(on_device, mesh.shape["gx"], mesh.shape["gy"])
    return jax.shard_map(body, mesh=mesh, in_specs=in_specs, out_specs=out_specs, check_vma=False)
```

```python
import functools

import jax
import jax.numpy as jnp
from jax import lax
from jax.experimental import pallas as pl
from jax.experimental.pallas import tpu as pltpu
from jax.sharding import PartitionSpec as P

rope_base = 500000.0
MIB = 1024 * 1024


def project_kernel(
    low, high, device_at, own, slab, head_dim, tokens_ref, wq_ref, wk_ref, wv_ref, keep_ref, *refs
):
    send_refs = refs[: low - 1]
    t_buf, q_buf, k_buf, v_buf, partial, sems = refs[low - 1 :]
    rows, depth = tokens_ref.shape
    heads = q_buf.shape[1] // head_dim
    kv_heads = wk_ref.shape[1] // head_dim
    t_copy = pltpu.make_async_copy(tokens_ref, t_buf, sems.at[0])
    k_copy = pltpu.make_async_copy(wk_ref, k_buf, sems.at[1])
    v_copy = pltpu.make_async_copy(wv_ref, v_buf, sems.at[2])
    t_copy.start(priority=1)
    k_copy.start(priority=1)
    v_copy.start(priority=1)
    q_copies = []
    for c in range(depth // slab):
        at = slice(c * slab, (c + 1) * slab)
        q_copies.append((pltpu.make_async_copy(wq_ref.at[at, :], q_buf.at[at, :], sems.at[3 + c]), at))
        q_copies[-1][0].start(priority=1)

    row = lax.broadcasted_iota(jnp.int32, (rows, rows), 0)
    column = lax.broadcasted_iota(jnp.int32, (rows, rows), 1)
    wanted = jnp.zeros((rows, rows), jnp.int32)
    for p in range(low):
        for q in range(high):
            at = p * high + q
            wanted = jnp.where(row >= at * own, row + (device_at(p, q) - at) * own, wanted)
    pick = (column == wanted).astype(jnp.bfloat16)
    t_copy.wait()
    tokens = jnp.dot(pick, t_buf[...], preferred_element_type=jnp.float32).astype(jnp.bfloat16)

    group = high * own

    def put(part, head):
        count = part.shape[1] // head_dim
        for p in range(low):
            ref = send_refs[p - 1] if p else keep_ref
            tiles = [
                part[p * group : (p + 1) * group, h * head_dim : (h + 1) * head_dim] for h in range(count)
            ]
            ref[head * group : (head + count) * group, :] = jnp.concatenate(tiles, axis=0).astype(ref.dtype)

    def times(part, weights):
        return jnp.dot(part, weights, preferred_element_type=jnp.float32)

    k_copy.wait()
    put(times(tokens, k_buf[...]), heads)
    v_copy.wait()
    put(times(tokens, v_buf[...]), heads + kv_heads)
    q_cols = q_buf.shape[1]
    width = q_cols // 4 if q_cols % (4 * head_dim) == 0 else q_cols
    for c, (copy, at) in enumerate(q_copies):
        copy.wait()
        for first in range(0, q_cols, width):
            columns = slice(first, first + width)
            part = times(tokens[:, at], q_buf[at, columns])
            if c > 0:
                part = part + partial[:, columns]
            if c < len(q_copies) - 1:
                partial[:, columns] = part
            else:
                put(part, first // head_dim)


def partner(f, k, count):
    return f ^ k if count & (count - 1) == 0 else (f + k) % count


def source(f, k, count):
    return f ^ k if count & (count - 1) == 0 else (f + count - k) % count


def combine_kernel(steps, heads, kv_heads, cache_ref, keep_ref, *refs):
    received, outs, total_ref = refs[: -steps - 1], refs[-steps - 1 : -1], refs[-1]
    total = keep_ref[...]
    for part in received:
        total = total + part[...].astype(jnp.float32)
    total_ref[: total.shape[0], :] = total
    own = outs[0].shape[0] // (heads + 2 * kv_heads)
    group = steps * own

    def of_heads(j, first, count):
        return [total_ref[pl.ds(first * group + j * own + r, count, stride=group), :] for r in range(own)]

    for j in range(steps):
        rows = (
            of_heads(j, 0, heads)
            + of_heads(j, heads, kv_heads)
            + of_heads(j, heads + kv_heads, kv_heads)
        )
        outs[j][...] = jnp.concatenate(rows, axis=0).astype(outs[j].dtype)


def attend_kernel(table_ref, keys, values, *refs):
    parts, out_ref = refs[:-1], refs[-1]
    rows, kv_heads, slots, head_dim = keys.shape
    heads = out_ref.shape[0] // rows
    group = heads // kv_heads
    pairs = [(r, k) for r in range(rows) for k in range(kv_heads)]
    total = parts[0][...].astype(jnp.float32)
    for part in parts[1:]:
        total = total + part[...].astype(jnp.float32)
    tile = table_ref.shape[0] // 3
    cosine = table_ref[:tile][:rows]
    sine = table_ref[tile : 2 * tile][:rows]
    filled = table_ref[2 * tile :][:rows]

    def rotated(vectors, count):
        per_row = (rows, count, head_dim)
        c = jnp.broadcast_to(cosine[:, None, :], per_row).reshape(rows * count, head_dim)
        s = jnp.broadcast_to(sine[:, None, :], per_row).reshape(rows * count, head_dim)
        return (vectors * c + pltpu.roll(vectors, head_dim // 2, 1) * s).astype(jnp.bfloat16)

    q_count = rows * heads
    kv_count = rows * kv_heads
    queries = rotated(total[:q_count], heads)
    new_keys = rotated(total[q_count : q_count + kv_count], kv_heads).astype(jnp.float32)
    new_values = total[q_count + kv_count :].astype(jnp.bfloat16).astype(jnp.float32)
    scaling = head_dim ** (-0.5)
    slot = lax.broadcasted_iota(jnp.int32, (group, slots), 1).astype(jnp.float32)
    scores = []
    own_scores = []
    for i, (r, k) in enumerate(pairs):
        q = queries[i * group : (i + 1) * group]
        score = lax.dot_general(
            q, keys[r, k], (((1,), (1,)), ((), ())), preferred_element_type=jnp.float32
        )
        scores.append(jnp.where(slot < filled[r : r + 1, :1], score * scaling, jnp.float32(-1e30)))
        own_scores.append(
            jnp.sum(q.astype(jnp.float32) * new_keys[i : i + 1], axis=1, keepdims=True) * scaling
        )
    highest = [
        jnp.maximum(jnp.max(score, axis=1, keepdims=True), own)
        for score, own in zip(scores, own_scores)
    ]
    weights = [jnp.exp(score - high) for score, high in zip(scores, highest)]
    own_weights = [jnp.exp(own - high) for own, high in zip(own_scores, highest)]
    norms = [
        jnp.sum(weight, axis=1, keepdims=True) + own for weight, own in zip(weights, own_weights)
    ]
    mixed = []
    for i, (r, k) in enumerate(pairs):
        head = jnp.dot(weights[i].astype(jnp.bfloat16), values[r, k], preferred_element_type=jnp.float32)
        mixed.append((head + own_weights[i] * new_values[i : i + 1]) / norms[i])
    out_ref[...] = jnp.concatenate(mixed, axis=0).astype(jnp.bfloat16)


def fill_rows(x):
    rows = x.shape[0]
    return jnp.concatenate([x] * (128 // rows), axis=0) if rows < 128 and 128 % rows == 0 else x


def output_kernel(gy, order, w_ref, *refs):
    low = len(order)
    blocks = refs[:low]
    own_ref, other_ref, wide, lhs = refs[low:]
    high, per_dev, head_dim = blocks[0].shape
    heads = w_ref.shape[0] // head_dim
    rows = high * low * per_dev // heads
    out_cols = w_ref.shape[1]
    width = min(512, out_cols)
    half = high * low // gy
    me, me_gy = lax.axis_index("gx"), lax.axis_index("gy")
    for k in range(low):
        for j in range(high):
            d = source(lax.div(me, low), j, high) * low + source(lax.rem(me, low), order[k], low)
            place = lax.rem(lax.div(d, half) + gy - me_gy, gy) * half + lax.rem(d, half)
            wide[pl.ds(pl.multiple_of(place * per_dev, per_dev), per_dev), :] = blocks[k][j].astype(jnp.float32)
    for h in range(heads):
        lhs[:, h * head_dim : (h + 1) * head_dim] = wide[pl.ds(h, rows, stride=heads), :].astype(lhs.dtype)
    filled = fill_rows(lhs[...])
    for c in range(out_cols // width):
        part = jnp.dot(
            filled, w_ref[:, c * width : (c + 1) * width], preferred_element_type=jnp.float32
        )
        own_ref[:, c * width : (c + 1) * width] = part[: rows // gy]
        for j in range(1, gy):
            other = part[j * (rows // gy) : (j + 1) * (rows // gy)]
            other_ref[j - 1, :, c * width : (c + 1) * width] = other.astype(other_ref.dtype)


def in_hbm(x):
    return pltpu.with_memory_space_constraint(x, pltpu.HBM)


def in_vmem(x):
    return pltpu.with_memory_space_constraint(x, pltpu.VMEM)


def on_device(n, gy, tokens, w_query, w_key, w_value, w_out, key_cache, value_cache, lengths):
    own_rows, kv_heads, slots, head_dim = key_cache.shape
    rows, depth = tokens.shape
    q_cols = w_query.shape[1]
    kv_cols = w_key.shape[1]
    heads = q_cols // head_dim
    out_cols = w_out.shape[1]
    vmem = pl.BlockSpec(memory_space=pltpu.VMEM)
    anywhere = pl.BlockSpec(memory_space=pl.ANY)
    block = own_rows * (heads + 2 * kv_heads)

    low = n
    while low * low >= 4 * n and low % 2 == 0:
        low //= 2
    high = n // low
    order = range(low - 1, 0, -1)

    def to_low(x, k):
        return lax.ppermute(
            x, "gx", [(h * low + i, h * low + int(partner(i, k, low))) for h in range(high) for i in range(low)]
        )

    def to_high(x, k):
        return lax.ppermute(
            x, "gx", [(h * low + i, int(partner(h, k, high)) * low + i) for h in range(high) for i in range(low)]
        )

    slab = 128 if depth % 128 == 0 else depth

    def device_at(p, q):
        me = lax.axis_index("gx")
        return partner(lax.div(me, low), q, high) * low + partner(lax.rem(me, low), p, low)

    all_heads = heads + 2 * kv_heads
    keep, *sends = pl.pallas_call(
        functools.partial(project_kernel, low, high, device_at, own_rows, slab, head_dim),
        out_shape=[
            jax.ShapeDtypeStruct(
                (all_heads * high * own_rows, head_dim), jnp.bfloat16 if p else jnp.float32
            )
            for p in range(low)
        ],
        in_specs=[anywhere, anywhere, anywhere, anywhere],
        out_specs=[vmem] * low,
        scratch_shapes=[
            pltpu.VMEM((rows, depth), jnp.bfloat16),
            pltpu.VMEM((depth, q_cols), jnp.bfloat16),
            pltpu.VMEM((depth, kv_cols), jnp.bfloat16),
            pltpu.VMEM((depth, kv_cols), jnp.bfloat16),
            pltpu.VMEM((rows, q_cols), jnp.float32),
            pltpu.SemaphoreType.DMA((3 + depth // slab,)),
        ],
        compiler_params=pltpu.CompilerParams(vmem_limit_bytes=26 * MIB),
        cost_estimate=pl.CostEstimate(
            flops=2 * rows * depth * (q_cols + 2 * kv_cols),
            bytes_accessed=2 * depth * (q_cols + 2 * kv_cols),
            transcendentals=0,
        ),
        name="project",
    )(in_hbm(tokens), in_hbm(w_query), in_hbm(w_key), in_hbm(w_value))

    received = [to_low(sends[p - 1], p) for p in order]

    summed = pl.pallas_call(
        functools.partial(combine_kernel, high, heads, kv_heads),
        out_shape=[
            jax.ShapeDtypeStruct((block, head_dim), jnp.bfloat16 if q else jnp.float32)
            for q in range(high)
        ],
        in_specs=[vmem] * (2 + len(received)),
        out_specs=[vmem] * high,
        scratch_shapes=[pltpu.VMEM(((all_heads + 8) * high * own_rows, head_dim), jnp.float32)],
        compiler_params=pltpu.CompilerParams(vmem_limit_bytes=12 * MIB),
        cost_estimate=pl.CostEstimate(flops=0, bytes_accessed=16 * MIB, transcendentals=0),
        name="combine",
    )(in_vmem(value_cache), keep, *received)

    parts = [summed[0]] + [to_high(summed[q], q) for q in range(1, high)]

    half = head_dim // 2
    freqs = rope_base ** (-2.0 * jnp.arange(half).astype(jnp.float32) / (2.0 * half))
    positions = jnp.pad(lengths.astype(jnp.float32), (0, -own_rows % 8))[:, None]
    angles = positions * freqs[None, :]
    cosine = jnp.cos(angles)
    sine = jnp.sin(angles)
    table = jnp.concatenate(
        [
            jnp.concatenate([cosine, cosine], axis=1),
            jnp.concatenate([-sine, sine], axis=1),
            jnp.broadcast_to(positions, (positions.shape[0], head_dim)),
        ],
        axis=0,
    )

    mixed = pl.pallas_call(
        attend_kernel,
        out_shape=jax.ShapeDtypeStruct((own_rows * heads, head_dim), jnp.bfloat16),
        in_specs=[vmem] * (3 + len(parts)),
        out_specs=vmem,
        compiler_params=pltpu.CompilerParams(vmem_limit_bytes=12 * MIB),
        cost_estimate=pl.CostEstimate(
            flops=4 * own_rows * heads * slots * head_dim,
            bytes_accessed=4 * own_rows * kv_heads * slots * head_dim,
            transcendentals=own_rows * heads * slots,
        ),
        name="attend",
    )(table, in_vmem(key_cache), in_vmem(value_cache), *parts)

    column = jnp.stack([mixed] + [to_high(mixed, q) for q in range(1, high)])
    blocks = [column] + [to_low(column, k) for k in order]

    own, other = pl.pallas_call(
        functools.partial(output_kernel, gy, (0, *order)),
        out_shape=(
            jax.ShapeDtypeStruct((rows // gy, out_cols), jnp.float32),
            jax.ShapeDtypeStruct((gy - 1, rows // gy, out_cols), jnp.bfloat16),
        ),
        in_specs=[vmem] * (1 + low),
        out_specs=(vmem, vmem),
        scratch_shapes=[
            pltpu.VMEM(((rows + 1) * heads, head_dim), jnp.float32),
            pltpu.VMEM((rows, q_cols), jnp.bfloat16),
        ],
        compiler_params=pltpu.CompilerParams(vmem_limit_bytes=12 * MIB),
        cost_estimate=pl.CostEstimate(
            flops=2 * rows * q_cols * out_cols,
            bytes_accessed=2 * q_cols * out_cols,
            transcendentals=0,
        ),
        name="output",
    )(in_vmem(w_out), *blocks)

    total = own
    for j in range(1, gy):
        part = lax.ppermute(other[j - 1], "gy", [(i, (i + j) % gy) for i in range(gy)])
        total = total + part.astype(jnp.float32)
    return total.astype(jnp.bfloat16)


def solution(mesh):
    in_specs = (
        P("groups", "gx"),
        P("gx", "gy"),
        P("gx", "gy"),
        P("gx", "gy"),
        P("gy", "gx"),
        P(("groups", "gx"), "gy", None, None),
        P(("groups", "gx"), "gy", None, None),
        P(("groups", "gx")),
    )
    out_specs = P(("groups", "gy"), "gx")
    body = functools.partial(on_device, mesh.shape["gx"], mesh.shape["gy"])
    return jax.shard_map(body, mesh=mesh, in_specs=in_specs, out_specs=out_specs, check_vma=False)
```
